128 devices in a mesh: inst: 8 (over x_hi, z), tp: 16 (over x_lo, y, core).
Axes of the slice: x: 4 (x_hi: 2, x_lo: 2; x = x_hi * 2 + x_lo), y: 4, z: 4, core: 2. Of those that a mesh axis runs over, the one named last changes fastest.
Arguments:
- prompt: bfloat16 [8192, 4096], P('inst', 'tp'), may hold values from -6 to 6
- decode_tokens: bfloat16 [2, 128, 4096], P(None, 'inst', 'tp'), may hold values from -6 to 6
- query_weight: bfloat16 [4096, 4096], P(None, 'tp'), as said below
- key_weight: bfloat16 [4096, 4096], P(None, 'tp'), as said below
- value_weight: bfloat16 [4096, 4096], P(None, 'tp'), may hold values from -0.09375 to 0.09375
- out_weight: bfloat16 [4096, 4096], P('tp'), may hold values from -0.09375 to 0.09375
- cache_keys: bfloat16 [128, 32, 16, 4096], P(None, 'inst', None, 'tp'), may hold values from -6 to 6
- cache_values: bfloat16 [128, 32, 16, 4096], P(None, 'inst', None, 'tp'), may hold values from -6 to 6
- stretch_lengths: int32 [8], replicated, may hold values from 1 to 1024, 6144 in all
- panel_map: int32 [128, 32], P(None, 'inst'), may hold values from 0 to 31, each once within a row
- ctx_lengths: int32 [128], replicated, may hold values from 1 to 512, 32768 in all
Outputs:
- prefill_out: float32 [8192, 4096], P('inst', 'tp')
- decode_out: float32 [2, 128, 4096], P(None, 'inst', 'tp')
The draws below stay inside these ranges and needn't reach their ends.
Inputs may be any that keep to these rules, and one draw needn't show every extreme that they name: `panel_map`: each row holds every panel number once. `query_weight`: scaled by the inverse square root of 4096. `key_weight`: scaled by the inverse square root of 4096.
All inputs are finite; a program needn't handle non-finite values.
Results may differ from the reference program's by a relative error of at most 0.01005.
Values may be sent and summed in bfloat16 or wider, within the bound.
No kernel may reach another device: no remote copies, remote signals or barrier semaphores. Data moves between devices by JAX's collectives and lax.ppermute only.
A program may use at most 128 MiB of HBM per device.

```python
import math
import jax
import jax.numpy as jnp
import numpy as np
from jax import lax

D = 4096
H = 32
HD = 128
CH = 1024
PANEL = 16
REQ = 128
STEPS = 2
SEQ = 8192
NPAN = 32
CTX = 512
N_INST = 8


def draw_query_weight(key, part):
    key = jax.random.fold_in(key, 11)
    own = jax.random.normal(key, (D, H * HD), jnp.float32)
    return (own / math.sqrt(D)).astype(jnp.bfloat16)


def draw_key_weight(key, part):
    key = jax.random.fold_in(key, 23)
    own = jax.random.normal(key, (D, H * HD), jnp.float32)
    return (own / math.sqrt(D)).astype(jnp.bfloat16)


def shard_levels(rng, extent, shards, low, high):
    def one(dim, parts):
        draws = jax.random.uniform(jax.random.fold_in(jax.random.fold_in(rng, 6), dim), (parts,), jnp.float32, low / len(shards), high / len(shards))
        return jnp.repeat(jnp.exp(draws), extent[dim] // parts).reshape((-1,) + (1,) * (len(extent) - dim - 1))

    loudness = one(*shards[0])
    for cut in shards[1:]:
        loudness = loudness * one(*cut)
    return loudness


def profile(number_of, total, limit, skew):
    portions = [(1 << 20) // math.isqrt(rank ** skew) + 1 for rank in range(2, number_of + 1)]
    rest, holding = total - limit - (number_of - 1), [1] * (number_of - 1)
    while rest > 0:
        candidates = [i for i in range(number_of - 1) if holding[i] < limit]
        pool, remaining = sum([portions[i] for i in candidates]), rest
        for i in candidates:
            extra = min(limit - holding[i], max(1, remaining * portions[i] // pool), rest)
            holding[i] = holding[i] + extra
            rest = rest - extra
    return np.array([limit] + holding)


def ragged_sizes(stream_key, number_of, total, reach, slope):
    if number_of == 2:
        one = jax.random.randint(stream_key, (), max(1, total - reach), min(reach, total - 1) + 1)
        return jnp.stack([one, total - one])
    lengths = jnp.asarray(profile(number_of, total, reach, slope), jnp.int32)
    twos = (number_of - 1) // 2
    source_of, taker = lengths[1:1 + 2 * twos:2], lengths[2:2 + 2 * twos:2]
    slack = jnp.minimum(source_of - 1, reach - taker)
    passed = jax.random.randint(jax.random.fold_in(stream_key, 1), (twos,), 0, 1 << 20) % (slack + 1)
    lengths = lengths.at[1:1 + 2 * twos:2].set(source_of - passed).at[2:2 + 2 * twos:2].set(taker + passed)
    return lengths[jax.random.permutation(jax.random.fold_in(stream_key, 2), number_of)]


def centred(own_key, shape, spread, reach, shards=(), held_as=jnp.bfloat16):
    loudness = shard_levels(own_key, shape, shards, -0.22, 0.18) if shards else 1.0
    result = jax.random.normal(own_key, shape, jnp.float32) * spread * loudness
    return jnp.minimum(jnp.maximum(result, -reach), reach).astype(held_as)


def setup_inputs(seed: int = 0) -> dict:
    seeds = jax.random.split(jax.random.key(seed), 12)
    prompt = centred(seeds[0], (SEQ, D), 1.0, 6.0, ((0, 8), (1, 16)))
    decode_tokens = centred(seeds[1], (STEPS, REQ, D), 1.0, 6.0, ((1, 8), (2, 16)))
    query_weight = draw_query_weight(jax.random.fold_in(seeds[11], 71), 0)
    key_weight = draw_key_weight(jax.random.fold_in(seeds[11], 71), 0)
    value_weight = centred(seeds[4], (D, H * HD), D ** -0.5, 0.09375, ((1, 16),))
    out_weight = centred(seeds[5], (H * HD, D), (H * HD) ** -0.5, 0.09375, ((0, 16),))
    cache_keys = centred(seeds[6], (REQ, NPAN, PANEL, H * HD), 1.0, 6.0, ((1, 8), (3, 16)))
    cache_values = centred(seeds[7], (REQ, NPAN, PANEL, H * HD), 1.0, 6.0, ((1, 8), (3, 16)))
    stretch_lengths = ragged_sizes(seeds[8], N_INST, N_INST * CH * 3 // 4, CH, 2).astype(jnp.int32)
    panel_map = jax.vmap(lambda own: jax.random.permutation(own, NPAN))(jax.random.split(seeds[9], REQ)).reshape((REQ, NPAN)).astype(jnp.int32)
    ctx_lengths = ragged_sizes(seeds[10], REQ, REQ * CTX // 2, CTX, 2).astype(jnp.int32)
    return dict(prompt=prompt, decode_tokens=decode_tokens, query_weight=query_weight, key_weight=key_weight, value_weight=value_weight, out_weight=out_weight, cache_keys=cache_keys, cache_values=cache_values, stretch_lengths=stretch_lengths, panel_map=panel_map, ctx_lengths=ctx_lengths)


NEGATIVE = -1e+30

def project(inputs, weight):
    return jnp.dot(inputs, weight, preferred_element_type=jnp.float32).astype(jnp.bfloat16)

def reference(prompt, decode_tokens, query_weight, key_weight, value_weight, out_weight, cache_keys, cache_values, stretch_lengths, panel_map, ctx_lengths):
    score_scale = 1.0 / math.sqrt(HD)
    pre_queries = project(prompt, query_weight).reshape(SEQ, H, HD).transpose(1, 0, 2)
    pre_keys = project(prompt, key_weight).reshape(SEQ, H, HD).transpose(1, 0, 2)
    pre_values = project(prompt, value_weight).reshape(SEQ, H, HD).transpose(1, 0, 2)
    slots = jnp.arange(SEQ, dtype=jnp.int32)
    source = slots // CH
    slot_used = slots - source * CH < stretch_lengths[source]
    allowed = slot_used[None, :] & (slots[None, :] <= slots[:, None])

    def prefill_head(inputs):
        query_head, key_head, value_head = inputs
        scores = jnp.dot(query_head, key_head.T, preferred_element_type=jnp.float32) * score_scale
        scores = jnp.where(allowed, scores, NEGATIVE)
        top_score = lax.optimization_barrier(jnp.max(scores, axis=1))
        weights = jnp.where(allowed, jnp.exp(scores - top_score[:, None]), 0.0)
        totals = lax.optimization_barrier(jnp.sum(weights, axis=1))
        output = jnp.dot(weights.astype(jnp.bfloat16), value_head, preferred_element_type=jnp.float32)
        return output / totals[:, None]
    pre_heads = lax.map(prefill_head, (pre_queries, pre_keys, pre_values))
    pre_attn = pre_heads.transpose(1, 0, 2).reshape(SEQ, H * HD)
    pre_attn = (pre_attn * slot_used[:, None].astype(jnp.float32)).astype(jnp.bfloat16)
    prefill_out = jnp.dot(pre_attn, out_weight, preferred_element_type=jnp.float32)
    flat_tokens = decode_tokens.reshape(STEPS * REQ, D)
    dec_queries = project(flat_tokens, query_weight).reshape(STEPS, REQ, H, HD).transpose(2, 0, 1, 3)
    dec_keys = project(flat_tokens, key_weight).reshape(STEPS, REQ, H, HD).transpose(2, 0, 1, 3)
    dec_values = project(flat_tokens, value_weight).reshape(STEPS, REQ, H, HD).transpose(2, 0, 1, 3)
    cache_key_heads = cache_keys.reshape(REQ, CTX, H, HD).transpose(2, 0, 1, 3)
    cache_value_heads = cache_values.reshape(REQ, CTX, H, HD).transpose(2, 0, 1, 3)
    positions = (panel_map[:, :, None] * PANEL + jnp.arange(PANEL, dtype=jnp.int32)[None, None, :]).reshape(REQ, CTX)
    cache_ok = positions < ctx_lengths[:, None]
    order_ok = jnp.arange(STEPS, dtype=jnp.int32)[None, :] <= jnp.arange(STEPS, dtype=jnp.int32)[:, None]

    def rounded(weights):
        return lax.optimization_barrier(weights.astype(jnp.bfloat16)).astype(jnp.float32)

    def decode_head(inputs):
        query_head, new_keys, new_values, key_head, value_head, cache_key_head, cache_value_head = inputs
        query_float = query_head.astype(jnp.float32)
        scores_pre = jnp.einsum('srd,jd->srj', query_float, key_head.astype(jnp.float32)) * score_scale
        scores_pre = jnp.where(slot_used[None, None, :], scores_pre, NEGATIVE)
        scores_cache = jnp.einsum('srd,rkd->srk', query_float, cache_key_head.astype(jnp.float32)) * score_scale
        scores_cache = jnp.where(cache_ok[None], scores_cache, NEGATIVE)
        scores_new = jnp.einsum('srd,urd->sru', query_float, new_keys.astype(jnp.float32)) * score_scale
        scores_new = jnp.where(order_ok[:, None, :], scores_new, NEGATIVE)
        top_score = jnp.maximum(jnp.maximum(lax.optimization_barrier(jnp.max(scores_pre, axis=-1)), lax.optimization_barrier(jnp.max(scores_cache, axis=-1))), lax.optimization_barrier(jnp.max(scores_new, axis=-1)))
        weight_pre = jnp.where(slot_used[None, None, :], jnp.exp(scores_pre - top_score[..., None]), 0.0)
        weight_cache = jnp.where(cache_ok[None], jnp.exp(scores_cache - top_score[..., None]), 0.0)
        weight_new = jnp.where(order_ok[:, None, :], jnp.exp(scores_new - top_score[..., None]), 0.0)
        totals = lax.optimization_barrier(jnp.sum(weight_pre, axis=-1)) + lax.optimization_barrier(jnp.sum(weight_cache, axis=-1)) + lax.optimization_barrier(jnp.sum(weight_new, axis=-1))
        output = jnp.einsum('srj,jd->srd', rounded(weight_pre), value_head.astype(jnp.float32))
        output = output + jnp.einsum('srk,rkd->srd', rounded(weight_cache), cache_value_head.astype(jnp.float32))
        output = output + jnp.einsum('sru,urd->srd', rounded(weight_new), new_values.astype(jnp.float32))
        return output / totals[..., None]
    dec_heads = lax.map(decode_head, (dec_queries, dec_keys, dec_values, pre_keys, pre_values, cache_key_heads, cache_value_heads))
    dec_attn = dec_heads.transpose(1, 2, 0, 3).reshape(STEPS * REQ, H * HD).astype(jnp.bfloat16)
    decode_out = jnp.dot(dec_attn, out_weight, preferred_element_type=jnp.float32).reshape(STEPS, REQ, D)
    return (prefill_out, decode_out)
```

```python
import functools
import math

import jax
import jax.numpy as jnp
from jax import lax
from jax.experimental import pallas as pl
from jax.experimental.pallas import tpu as pltpu
from jax.sharding import PartitionSpec as P

HD = 128
CH = 1024
PANEL = 16
STEPS = 2
NEGATIVE = -1e30
SCALE = math.log2(math.e) / math.sqrt(HD)
AX = ("inst", "tp")
HALF = 512
GROUP = 256
DEC = 16
ROWS = HALF + DEC
CUT = 256
BF = jnp.bfloat16
F32 = jnp.float32
MIB = 1 << 20


def perm(dxh=0, dz=0, dxl=0, dy=0, dc=0, only_xh=None, zxor=0):
    pairs = []
    for xh in range(2):
        if only_xh is not None and xh != only_xh:
            continue
        for z in range(4):
            for xl in range(2):
                for y in range(4):
                    for c in range(2):
                        source = (xh * 4 + z) * 16 + xl * 8 + y * 2 + c
                        target = (
                            ((xh ^ dxh) * 4 + (((z + dz) % 4) ^ zxor)) * 16
                            + (xl ^ dxl) * 8
                            + ((y + dy) % 4) * 2
                            + (c ^ dc)
                        )
                        pairs.append((source, target))
    return pairs


def move(x, **steps):
    return lax.ppermute(x, AX, perm(**steps))


def gather_chips(own):
    before = move(own, dy=1)
    after = move(own, dy=-1)
    beside = move(own, dxl=1)
    far_lo = move(before[:CUT], dy=1)
    far_hi = move(after[CUT:], dy=-1)
    before_hi = move(beside[CUT:], dy=1)
    after_hi = move(beside[CUT:], dy=-1)
    before_lo = move(before[:CUT], dxl=1)
    after_lo = move(after[:CUT], dxl=1)
    far2_lo = move(before_lo, dy=1)
    far2_hi = move(after_hi, dy=-1)
    return (
        own, before, after, beside,
        far_lo, far_hi, before_lo, before_hi, after_lo, after_hi, far2_lo, far2_hi,
    )


PLACES = (
    (0, 0, None), (0, -1, None), (0, 1, None), (1, 0, None),
    (0, 2, 0), (0, 2, 1), (1, -1, 0), (1, -1, 1), (1, 1, 0), (1, 1, 1), (1, 2, 0), (1, 2, 1),
)


def chip_at(idx, dx, dy):
    x = idx[2]
    x = 1 - x if dx else x
    return x * 4 + lax.rem(idx[3] + dy + 4, 4)


def part_rows(part, rows):
    return (0, rows) if part is None else ((0, CUT) if part == 0 else (CUT, rows - CUT))


def qkv_kernel(idx, *refs):
    pieces, weights = refs[:12], refs[12:18]
    y_ref, z_ref, xs, ws, sems = refs[18:]
    core, z = idx[0], idx[1]
    copies = []
    for piece, (dx, dy, part) in zip(pieces, PLACES):
        start, size = part_rows(part, ROWS)
        chip = chip_at(idx, dx, dy)
        for half in range(2):
            side = core if half == 0 else 1 - core
            column = pl.multiple_of(chip * 512 + side * 256, 256)
            copies.append(
                pltpu.make_async_copy(
                    piece.at[:, pl.ds(half * 256, 256)],
                    xs.at[pl.ds(start, size), pl.ds(column, 256)],
                    sems.at[6 + len(copies)],
                )
            )
    loads = [
        pltpu.make_async_copy(weights[n], ws.at[n], sems.at[n]) for n in range(6)
    ]
    for copy in copies:
        copy.start()
    for load in loads:
        load.start()
    for copy in copies:
        copy.wait()
    for n in range(6):
        loads[n].wait()
        rel, kind = n // 3, n % 3
        owner = core if rel == 0 else 1 - core
        result = jnp.dot(xs[...], ws[n], preferred_element_type=F32)
        if kind == 0:
            result = result * SCALE
        result = result.astype(BF)
        y_ref[rel, :, kind * 256 : (kind + 1) * 256] = result
        for head in range(2):
            slot = lax.rem(owner * 2 + head - z + 4, 4)
            z_ref[slot, :, kind * 128 : (kind + 1) * 128] = result[
                :HALF, head * 128 : (head + 1) * 128
            ]


def any_spec():
    return pl.BlockSpec(memory_space=pl.ANY)


def vmem_spec():
    return pl.BlockSpec(memory_space=pltpu.VMEM)


def smem_spec():
    return pl.BlockSpec(memory_space=pltpu.SMEM)


def qkv(idx, pieces, weights):
    return pl.pallas_call(
        qkv_kernel,
        out_shape=(
            jax.ShapeDtypeStruct((2, ROWS, 768), BF),
            jax.ShapeDtypeStruct((4, HALF, 384), BF),
        ),
        in_specs=[smem_spec()] + [any_spec()] * 18,
        out_specs=(vmem_spec(), vmem_spec()),
        scratch_shapes=[
            pltpu.VMEM((ROWS, 4096), BF),
            pltpu.VMEM((6, 4096, 256), BF),
            pltpu.SemaphoreType.DMA((30,)),
        ],
        compiler_params=pltpu.CompilerParams(vmem_limit_bytes=34 * MIB),
        cost_estimate=pl.CostEstimate(
            flops=2 * ROWS * 4096 * 1536, bytes_accessed=20 * MIB, transcendentals=0
        ),
        name="qkv",
    )(idx, *pieces, *weights)


QT = 256
KT = 512


def attend_kernel(
    idx, lens, own, one, two, three, sib, cross, cross_sib, o_ref, ks, vs, m_ref, acc_ref
):
    core, z, xh = idx[0], idx[1], idx[4]
    blocks = (own, one, two, three)

    def place(slot, keys, values, side, first):
        for g in range(2):
            row = pl.multiple_of(g * 512 + side * 256, 256)
            ks[slot, pl.ds(row, 256), :] = keys[g * 256 : (g + 1) * 256]
            vs[slot, pl.ds(row, 256), :128] = values[g * 256 : (g + 1) * 256]
        if first:
            vs[slot, :, 128:] = jnp.ones((CH, 128), BF)

    for k in range(4):
        rows = slice(k * HALF, (k + 1) * HALF)
        place(k, blocks[k][:, 128:256], blocks[k][:, 256:384], core, True)
        place(k, sib[rows, :128], sib[rows, 128:], 1 - core, False)

    @pl.when(xh == 1)
    def _():
        for k in range(4):
            rows = slice(k * HALF, (k + 1) * HALF)
            place(4 + k, cross[rows, :128], cross[rows, 128:], core, True)
            place(4 + k, cross_sib[rows, :128], cross_sib[rows, 128:], 1 - core, False)

    def block_of(k):
        return lax.rem(z - k + 4, 4)

    for i in range(4):
        block = block_of(i)
        used = lens[xh * 4 + block]
        for g in range(2):
            first = g * 512 + core * 256
            rows = slice(g * 256, (g + 1) * 256)

            @pl.when(first < used)
            def _():
                q = blocks[i][rows, :128]
                m_ref[...] = jnp.full((QT, 128), NEGATIVE, F32)
                acc_ref[...] = jnp.zeros((QT, 256), F32)

                def step(slot, t, limit, causal):
                    start = pl.multiple_of(t * KT, KT)
                    keys = ks[slot, pl.ds(start, KT), :]
                    values = vs[slot, pl.ds(start, KT), :]
                    s = lax.dot_general(
                        q, keys, (((1,), (1,)), ((), ())), preferred_element_type=F32
                    )
                    if limit is not None:
                        key = start + lax.broadcasted_iota(jnp.int32, (QT, KT), 1)
                        allowed = key < limit
                        if causal:
                            row = first + lax.broadcasted_iota(jnp.int32, (QT, KT), 0)
                            allowed = allowed & (key <= row)
                        s = jnp.where(allowed, s, NEGATIVE)
                    old = m_ref[:, :1]
                    new = jnp.maximum(old, jnp.max(s, axis=1, keepdims=True))
                    p = jnp.exp2(s - new).astype(BF)
                    acc_ref[...] = acc_ref[...] * jnp.exp2(old - new) + jnp.dot(
                        p, values, preferred_element_type=F32
                    )
                    m_ref[...] = jnp.broadcast_to(new, (QT, 128))

                def sweep(slot, count):
                    whole = count // KT
                    lax.fori_loop(0, whole, lambda t, _: step(slot, t, None, False), None)

                    @pl.when(whole * KT < count)
                    def _():
                        step(slot, whole, count, False)

                tiles = (jnp.minimum(first + QT, used) + KT - 1) // KT
                lax.fori_loop(0, tiles, lambda t, _: step(i, t, used, True), None)

                def earlier(k, _):
                    other = block_of(k)

                    @pl.when(other < block)
                    def _():
                        sweep(k, lens[xh * 4 + other])

                    return None

                lax.fori_loop(0, 4, earlier, None)

                @pl.when(xh == 1)
                def _():
                    def crossed(k, _):
                        sweep(4 + k, lens[block_of(k)])
                        return None

                    lax.fori_loop(0, 4, crossed, None)

                row = first + lax.broadcasted_iota(jnp.int32, (QT, 128), 0)
                out = acc_ref[:, :128] / acc_ref[:, 128:]
                o_ref[i, rows, :] = jnp.where(row < used, out, 0.0).astype(BF)

            @pl.when(first >= used)
            def _():
                o_ref[i, rows, :] = jnp.zeros((QT, 128), BF)


def attend(idx, lens, pieces, sib, cross, cross_sib):
    return pl.pallas_call(
        attend_kernel,
        out_shape=jax.ShapeDtypeStruct((4, HALF, 128), BF),
        in_specs=[smem_spec()] * 2 + [vmem_spec()] * 7,
        out_specs=vmem_spec(),
        scratch_shapes=[
            pltpu.VMEM((8, CH, 128), BF),
            pltpu.VMEM((8, CH, 256), BF),
            pltpu.VMEM((QT, 128), F32),
            pltpu.VMEM((QT, 256), F32),
        ],
        compiler_params=pltpu.CompilerParams(vmem_limit_bytes=30 * MIB),
        cost_estimate=pl.CostEstimate(
            flops=12 * CH * CH * 512, bytes_accessed=4 * MIB, transcendentals=12 * CH * CH
        ),
        name="attend",
    )(idx, lens, *pieces, sib, cross, cross_sib)


def decode_kernel(idx, lens, q_ref, k_ref, v_ref, ok_ref, own, sib, out_ref):
    core, me = idx[0], idx[5]
    used = lens[me]
    keys_c = k_ref[...].reshape(CH, 256)
    values_c = v_ref[...].reshape(CH, 256)
    row = lax.broadcasted_iota(jnp.int32, (32, CH), 0)
    key = lax.broadcasted_iota(jnp.int32, (32, CH), 1)
    request = (row // 16) * 8 + row % 8
    ok_cache = (request == key // 64) & (ok_ref[0] > 0)
    at = lax.broadcasted_iota(jnp.int32, (32, HALF), 1)
    slot = (at // 256) * 512 + at % 256
    ok_own = slot + core * 256 < used
    ok_sib = slot + (1 - core) * 256 < used
    stats = []
    nt = (((1,), (1,)), ((), ()))
    for head in range(2):
        cols = slice(head * 128, (head + 1) * 128)
        kcols = slice(256 + head * 128, 256 + (head + 1) * 128)
        vcols = slice(512 + head * 128, 512 + (head + 1) * 128)
        q = q_ref[0][:, cols]
        s_c = lax.dot_general(q, keys_c[:, cols], nt, preferred_element_type=F32)
        s_o = lax.dot_general(q, own[:HALF, kcols], nt, preferred_element_type=F32)
        s_s = lax.dot_general(q, sib[:HALF, kcols], nt, preferred_element_type=F32)
        s_c = jnp.where(ok_cache, s_c, NEGATIVE)
        s_o = jnp.where(ok_own, s_o, NEGATIVE)
        s_s = jnp.where(ok_sib, s_s, NEGATIVE)
        top = jnp.maximum(
            jnp.max(s_c, axis=1, keepdims=True),
            jnp.maximum(
                jnp.max(s_o, axis=1, keepdims=True), jnp.max(s_s, axis=1, keepdims=True)
            ),
        )
        p_c = jnp.exp2(s_c - top)
        p_o = jnp.exp2(s_o - top)
        p_s = jnp.exp2(s_s - top)
        total = (
            jnp.sum(p_c, axis=1, keepdims=True)
            + jnp.sum(p_o, axis=1, keepdims=True)
            + jnp.sum(p_s, axis=1, keepdims=True)
        )
        out_ref[0, :, cols] = (
            jnp.dot(p_c.astype(BF), values_c[:, cols], preferred_element_type=F32)
            + jnp.dot(p_o.astype(BF), own[:HALF, vcols], preferred_element_type=F32)
            + jnp.dot(p_s.astype(BF), sib[:HALF, vcols], preferred_element_type=F32)
        )
        stats += [top, total]
    lane = lax.broadcasted_iota(jnp.int32, (32, 128), 1)
    out_ref[0, :, 256:] = jnp.where(
        lane < 32, stats[0], jnp.where(lane < 64, stats[1], jnp.where(lane < 96, stats[2], stats[3]))
    )


def decode_parts(idx, lens, queries, cache_keys, cache_values, ok, own, sib):
    def mine(m, idx, lens):
        return idx[5] ^ m

    return pl.pallas_call(
        decode_kernel,
        out_shape=jax.ShapeDtypeStruct((8, 32, 384), F32),
        grid_spec=pltpu.PrefetchScalarGridSpec(
            num_scalar_prefetch=2,
            grid=(8,),
            in_specs=[
                pl.BlockSpec((1, 32, 256), lambda m, idx, lens: (m, 0, 0)),
                pl.BlockSpec((16, 4, 16, 256), lambda m, idx, lens: (idx[5] ^ m, 0, 0, 0)),
                pl.BlockSpec((16, 4, 16, 256), lambda m, idx, lens: (idx[5] ^ m, 0, 0, 0)),
                pl.BlockSpec((1, 1, CH), lambda m, idx, lens: (idx[5] ^ m, 0, 0)),
                pl.BlockSpec((ROWS, 768), lambda m, idx, lens: (0, 0)),
                pl.BlockSpec((ROWS, 768), lambda m, idx, lens: (0, 0)),
            ],
            out_specs=pl.BlockSpec((1, 32, 384), lambda m, idx, lens: (m, 0, 0)),
        ),
        compiler_params=pltpu.CompilerParams(vmem_limit_bytes=20 * MIB),
        cost_estimate=pl.CostEstimate(
            flops=8 * 32 * 2048 * 1024, bytes_accessed=10 * MIB, transcendentals=8 * 64 * 2048
        ),
        name="decode_parts",
    )(idx, lens, queries, cache_keys, cache_values, ok, own, sib)


def merge_kernel(parts, qkv_rows, out_ref):
    for head in range(2):
        cols = slice(head * 128, (head + 1) * 128)
        tops = [parts[n, :, 256 + head * 64 : 256 + head * 64 + 1] for n in range(8)]
        sums = [parts[n, :, 288 + head * 64 : 288 + head * 64 + 1] for n in range(8)]
        for side in range(2):
            for s in range(2):
                rows = slice(side * 16 + s * 8, side * 16 + s * 8 + 8)
                q = qkv_rows[rows, cols].astype(F32)
                fresh = []
                for u in range(s + 1):
                    from_rows = slice(side * 16 + u * 8, side * 16 + u * 8 + 8)
                    k = qkv_rows[from_rows, 256 + head * 128 : 384 + head * 128].astype(F32)
                    v = qkv_rows[from_rows, 512 + head * 128 : 640 + head * 128].astype(F32)
                    fresh.append((jnp.sum(q * k, axis=1, keepdims=True), v))
                top = fresh[0][0]
                for score, _ in fresh[1:]:
                    top = jnp.maximum(top, score)
                for part in tops:
                    top = jnp.maximum(top, part[rows])
                total = jnp.zeros((8, 1), F32)
                out = jnp.zeros((8, 128), F32)
                for score, v in fresh:
                    w = jnp.exp2(score - top)
                    total += w
                    out += w.astype(BF).astype(F32) * v
                for n in range(8):
                    w = jnp.exp2(tops[n][rows] - top)
                    total += w * sums[n][rows]
                    out += w * parts[n, rows, cols]
                out_ref[rows, cols] = (out / total).astype(BF)


def merge_parts(parts, qkv_rows):
    return pl.pallas_call(
        merge_kernel,
        out_shape=jax.ShapeDtypeStruct((32, 256), BF),
        in_specs=[vmem_spec()] * 2,
        out_specs=vmem_spec(),
        cost_estimate=pl.CostEstimate(flops=MIB, bytes_accessed=MIB, transcendentals=1000),
        name="merge_parts",
    )(parts, qkv_rows)


def head_order_kernel(idx, a, b, c, d, out_ref):
    for k, piece in enumerate((a, b, c, d)):
        column = pl.multiple_of(lax.rem(idx[1] + k, 4) * 128, 128)
        out_ref[:, pl.ds(column, 128)] = piece[...]


def head_order(idx, pieces):
    return pl.pallas_call(
        head_order_kernel,
        out_shape=jax.ShapeDtypeStruct((HALF, 512), BF),
        in_specs=[smem_spec()] + [vmem_spec()] * 4,
        out_specs=vmem_spec(),
        cost_estimate=pl.CostEstimate(flops=0, bytes_accessed=MIB, transcendentals=0),
        name="head_order",
    )(idx, *pieces)


def out_kernel(idx, *refs):
    pieces = refs[:12]
    dec, w_own, w_sib, own_ref, sib_ref, dec_ref, xs, ws, sems = refs[12:]
    core = idx[0]
    copies = []
    for piece, (dx, dy, part) in zip(pieces, PLACES):
        start, size = part_rows(part, HALF)
        column = pl.multiple_of(chip_at(idx, dx, dy) * 512, 512)
        copies.append(
            pltpu.make_async_copy(
                piece, xs.at[pl.ds(start, size), pl.ds(column, 512)], sems.at[len(copies)]
            )
        )
    copies.append(
        pltpu.make_async_copy(dec, xs.at[pl.ds(HALF, 32), :], sems.at[len(copies)])
    )
    for k in range(8):
        chip = chip_at(idx, k // 4, -(k % 4))
        for w, side in ((w_own, core), (w_sib, 1 - core)):
            row = pl.multiple_of(chip * 512 + side * 256, 256)
            copies.append(
                pltpu.make_async_copy(
                    w.at[k], ws.at[pl.ds(row, 256), :], sems.at[len(copies)]
                )
            )
    for copy in copies:
        copy.start()
    for copy in copies:
        copy.wait()
    for rel in range(2):
        column = core if rel == 0 else 1 - core
        column = pl.multiple_of(column * 256, 256)
        result = jnp.dot(xs[...], ws[:, pl.ds(column, 256)], preferred_element_type=F32)
        if rel == 0:
            own_ref[...] = result[:HALF]
            dec_ref[...] = result[HALF:]
        else:
            sib_ref[...] = result[:HALF]


def out_project(idx, pieces, dec, w_own, w_sib):
    return pl.pallas_call(
        out_kernel,
        out_shape=(
            jax.ShapeDtypeStruct((HALF, 256), F32),
            jax.ShapeDtypeStruct((HALF, 256), F32),
            jax.ShapeDtypeStruct((32, 256), F32),
        ),
        in_specs=[smem_spec()] + [any_spec()] * 15,
        out_specs=(vmem_spec(), vmem_spec(), vmem_spec()),
        scratch_shapes=[
            pltpu.VMEM((HALF + 32, 4096), BF),
            pltpu.VMEM((4096, 512), BF),
            pltpu.SemaphoreType.DMA((29,)),
        ],
        compiler_params=pltpu.CompilerParams(vmem_limit_bytes=24 * MIB),
        cost_estimate=pl.CostEstimate(
            flops=2 * HALF * 4096 * 512, bytes_accessed=9 * MIB, transcendentals=0
        ),
        name="out_project",
    )(idx, *pieces, dec, w_own, w_sib)


def pick(pair, core):
    return jnp.where(core == 0, pair[0], pair[1])


def shards(
    prompt,
    decode_tokens,
    query_weight,
    key_weight,
    value_weight,
    out_weight,
    cache_keys,
    cache_values,
    stretch_lengths,
    panel_map,
    ctx_lengths,
):
    inst = lax.axis_index("inst")
    tp = lax.axis_index("tp")
    core = tp % 2
    y = (tp // 2) % 4
    x = tp // 8
    z = inst % 4
    xh = inst // 4
    idx = jnp.stack([core, z, x, y, xh, inst, 0, 0]).astype(jnp.int32)

    groups = prompt.reshape(2, 2, GROUP, 256)
    tokens = decode_tokens.reshape(STEPS, 2, 8, 256)
    halves = [
        jnp.concatenate(
            [groups[:, n].reshape(HALF, 256), tokens[:, n].reshape(DEC, 256)], axis=0
        )
        for n in range(2)
    ]
    mine, theirs = pick(halves, core), pick(halves[::-1], core)
    received = move(theirs, dc=1)
    block = jnp.concatenate([mine, received], axis=1)

    weights = (query_weight, key_weight, value_weight)
    sib_weights = tuple(move(w, dc=1) for w in weights)
    pieces = gather_chips(block)
    by_owner, by_head = qkv(idx, pieces, weights + sib_weights)

    own = by_head[0]
    one = move(by_head[1], dz=1)
    three = move(by_head[3], dz=3)
    two = move(by_head[2], dz=2)
    crossing = [
        move(by_head[k, :, 128:], dxh=1, dz=k, only_xh=0) for k in range(4)
    ]
    own_half = jnp.concatenate([a[:, 128:] for a in (own, one, two, three)], axis=0)
    sib_half = move(own_half, dc=1)
    cross = jnp.concatenate(crossing, axis=0)
    cross_sib = move(cross, dc=1)

    from_sib = move(by_owner[1], dc=1)
    own_rows = by_owner[0]
    first = jnp.where(core == 0, own_rows[HALF:], from_sib[HALF:])
    second = jnp.where(core == 0, from_sib[HALF:], own_rows[HALF:])
    dec_rows = jnp.concatenate([first, second], axis=0)
    queries = dec_rows[None, :, :256]
    queries = jnp.concatenate([queries, move(queries, zxor=1)], axis=0)
    queries = jnp.concatenate([queries, move(queries, dz=2)], axis=0)
    queries = jnp.concatenate([queries, move(queries, dxh=1)], axis=0)

    positions = (
        panel_map[:, :, None] * PANEL + jnp.arange(PANEL, dtype=jnp.int32)[None, None, :]
    )
    ok = (positions < ctx_lengths[:, None, None]).astype(F32).reshape(8, 1, CH)
    parts = decode_parts(
        idx, stretch_lengths, queries, cache_keys, cache_values, ok, own_rows, from_sib
    )
    moved = move(parts[4:], dxh=1)
    parts = jnp.concatenate([parts[:4], moved], axis=0).reshape(2, 2, 2, 32, 384)
    moved = move(parts[:, 1], dz=2)
    parts = jnp.stack([parts[:, 0], moved], axis=1).reshape(4, 2, 32, 384)
    moved = move(parts[:, 1], zxor=1)
    parts = jnp.stack([parts[:, 0], moved], axis=1).reshape(8, 32, 384)
    dec_attn = merge_parts(parts, dec_rows)
    dec_all = lax.all_gather(dec_attn, "tp", axis=1, tiled=True)

    out_w, by_head = lax.optimization_barrier((out_weight, by_head))
    spread = []
    for k in range(8):
        dx, dy = k // 4, k % 4
        target = (x ^ dx) * 4 + (y + dy) % 4
        columns = lax.dynamic_slice_in_dim(out_w, target * 512, 512, axis=1)
        spread.append(columns if k == 0 else move(columns, dxl=dx, dy=dy))
    w_own = jnp.stack(spread)
    w_sib = move(w_own, dc=1)

    heads = attend(
        idx, stretch_lengths, (own, one, two, three), sib_half, cross, cross_sib
    )
    back = (heads[0], move(heads[1], dz=3), move(heads[2], dz=2), move(heads[3], dz=1))
    attn = gather_chips(head_order(idx, back))
    mine, theirs, decode = out_project(idx, attn, dec_all, w_own, w_sib)
    received = move(theirs, dc=1)
    mine, received = mine.reshape(2, GROUP, 256), received.reshape(2, GROUP, 256)
    prefill_out = jnp.stack(
        [pick((mine, received), core), pick((received, mine), core)], axis=1
    ).reshape(CH, 256)
    decode_out = decode.reshape(2, STEPS, 8, 256).transpose(1, 0, 2, 3).reshape(STEPS, 16, 256)
    return prefill_out, decode_out


def solution(mesh):
    return jax.shard_map(
        shards,
        mesh=mesh,
        in_specs=(
            P("inst", "tp"),
            P(None, "inst", "tp"),
            P(None, "tp"),
            P(None, "tp"),
            P(None, "tp"),
            P("tp", None),
            P(None, "inst", None, "tp"),
            P(None, "inst", None, "tp"),
            P(),
            P(None, "inst"),
            P(),
        ),
        out_specs=(P("inst", "tp"), P(None, "inst", "tp")),
        check_vma=False,
    )
```

```python
import functools
import math

import jax
import jax.numpy as jnp
from jax import lax
from jax.experimental import pallas as pl
from jax.experimental.pallas import tpu as pltpu
from jax.sharding import PartitionSpec as P

HD = 128
CH = 1024
PANEL = 16
STEPS = 2
NEGATIVE = -1e30
SCALE = math.log2(math.e) / math.sqrt(HD)
AX = ("inst", "tp")
HALF = 512
GROUP = 256
DEC = 16
ROWS = HALF + DEC
CUT = 256
BF = jnp.bfloat16
F32 = jnp.float32
MIB = 1 << 20


def perm(dxh=0, dz=0, dxl=0, dy=0, dc=0, only_xh=None, zxor=0):
    pairs = []
    for xh in range(2):
        if only_xh is not None and xh != only_xh:
            continue
        for z in range(4):
            for xl in range(2):
                for y in range(4):
                    for c in range(2):
                        source = (xh * 4 + z) * 16 + xl * 8 + y * 2 + c
                        target = (
                            ((xh ^ dxh) * 4 + (((z + dz) % 4) ^ zxor)) * 16
                            + (xl ^ dxl) * 8
                            + ((y + dy) % 4) * 2
                            + (c ^ dc)
                        )
                        pairs.append((source, target))
    return pairs


def move(x, **steps):
    return lax.ppermute(x, AX, perm(**steps))


LOW = slice(0, CUT)
HIGH = ROWS - CUT


def gather_first(own):
    return own, move(own, dy=1), move(own, dy=-1), move(own, dxl=1)


def gather_second(first):
    _, before, after, beside = first
    up = move(jnp.concatenate([before[LOW], beside[CUT:]]), dy=1)
    down = move(jnp.concatenate([after[CUT:], beside[CUT:]]), dy=-1)
    across = move(jnp.concatenate([before[LOW], after[LOW]]), dxl=1)
    return up, down, across


def gather_third(second):
    _, down, across = second
    return move(across[LOW], dy=1), move(down[HIGH:], dy=-1)


STEPS_OF = (
    (
        ((0, 0), (0, -1), (0, 1), (1, 0)),
        tuple((n, 0, n, 0, ROWS) for n in range(4)),
    ),
    (
        ((0, 2), (1, -1), (1, 1)),
        (
            (0, 0, 0, 0, CUT), (0, CUT, 1, CUT, HIGH),
            (1, 0, 0, CUT, HIGH), (1, HIGH, 2, CUT, HIGH),
            (2, 0, 1, 0, CUT), (2, CUT, 2, 0, CUT),
        ),
    ),
    (((1, 2),), ((0, 0, 0, 0, CUT), (1, 0, 0, CUT, HIGH))),
)


def chip_at(idx, dx, dy):
    x = idx[2]
    x = 1 - x if dx else x
    return x * 4 + lax.rem(idx[3] + dy + 4, 4)


def qkv_kernel(step, idx, *refs):
    chips, parts = STEPS_OF[step]
    count = (4, 3, 2)[step]
    pieces, weights, refs = refs[:count], refs[count : count + 6], refs[count + 6 :]
    total, refs = (refs[0], refs[1:]) if step else (None, refs)
    xs, ws, sems = refs[-3:]
    core, z = idx[0], idx[1]
    copies = []
    for n in range(6):
        for place, (dx, dy) in enumerate(chips):
            rows = pl.ds(pl.multiple_of(chip_at(idx, dx, dy) * 512, 512), 512)
            copies.append(
                pltpu.make_async_copy(
                    weights[n].at[rows, :],
                    ws.at[n, pl.ds(place * 512, 512), :],
                    sems.at[len(copies)],
                )
            )
    for copy in copies:
        copy.start()
    for n, row, place, start, size in parts:
        for half in range(2):
            side = core if half == 0 else 1 - core
            column = pl.multiple_of(place * 512 + side * 256, 256)
            xs[start : start + size, pl.ds(column, 256)] = pieces[n][
                row : row + size, half * 256 : (half + 1) * 256
            ]
    for n in range(6):
        for place in range(len(chips)):
            copies[n * len(chips) + place].wait()
        result = jnp.dot(xs[...], ws[n], preferred_element_type=F32)
        if total is not None:
            result += total[n]
        if step < 2:
            refs[0][n] = result
            continue
        y_ref, z_ref = refs[:2]
        rel, kind = n // 3, n % 3
        owner = core if rel == 0 else 1 - core
        if kind == 0:
            result = result * SCALE
        result = result.astype(BF)
        y_ref[rel, :, kind * 256 : (kind + 1) * 256] = result
        for head in range(2):
            slot = lax.rem(owner * 2 + head - z + 4, 4)
            z_ref[slot, :HALF, kind * 128 : (kind + 1) * 128] = result[
                :HALF, head * 128 : (head + 1) * 128
            ]
        if kind == 0:
            for slot in range(4):
                z_ref[slot, HALF + rel * DEC : HALF + (rel + 1) * DEC, :256] = result[HALF:]
                z_ref[slot, HALF + rel * DEC : HALF + (rel + 1) * DEC, 256:] = result[HALF:, :128]


def vmem_spec():
    return pl.BlockSpec(memory_space=pltpu.VMEM)


def smem_spec():
    return pl.BlockSpec(memory_space=pltpu.SMEM)


def qkv(step, idx, pieces, weights, total=()):
    chips = len(STEPS_OF[step][0])
    shape = jax.ShapeDtypeStruct((6, ROWS, 256), F32)
    if step == 2:
        shape = (
            jax.ShapeDtypeStruct((2, ROWS, 768), BF),
            jax.ShapeDtypeStruct((4, HALF + 2 * DEC, 384), BF),
        )
    return pl.pallas_call(
        functools.partial(qkv_kernel, step),
        out_shape=shape,
        in_specs=[smem_spec()]
        + [vmem_spec()] * len(pieces)
        + [pl.BlockSpec(memory_space=pltpu.HBM)] * 6
        + [vmem_spec()] * len(total),
        out_specs=(vmem_spec(), vmem_spec()) if step == 2 else vmem_spec(),
        scratch_shapes=[
            pltpu.VMEM((ROWS, chips * 512), BF),
            pltpu.VMEM((6, chips * 512, 256), BF),
            pltpu.SemaphoreType.DMA((6 * chips,)),
        ],
        compiler_params=pltpu.CompilerParams(vmem_limit_bytes=56 * MIB),
        cost_estimate=pl.CostEstimate(
            flops=2 * ROWS * 512 * chips * 1536, bytes_accessed=8 * MIB, transcendentals=0
        ),
        name="qkv",
    )(idx, *pieces, *weights, *total)


def pack_kernel(a, b, c, d, out_ref):
    for n, piece in enumerate((a, b, c, d)):
        out_ref[n * HALF : (n + 1) * HALF, :] = piece[:HALF, 128:]


def pack(pieces):
    return pl.pallas_call(
        pack_kernel,
        out_shape=jax.ShapeDtypeStruct((4 * HALF, 256), BF),
        in_specs=[vmem_spec()] * 4,
        out_specs=vmem_spec(),
        compiler_params=pltpu.CompilerParams(vmem_limit_bytes=8 * MIB),
        cost_estimate=pl.CostEstimate(flops=0, bytes_accessed=4 * MIB, transcendentals=0),
        name="pack",
    )(*pieces)


QT = 256
KT = 1024
PACKED = 5 * CH + 256


def wide(a, n):
    return jnp.concatenate([a] * n, axis=1)


def place_keys(idx, lens, base, mine, sib, ks, vs, offs):
    core, z = idx[0], idx[1]

    def block(b, offset):
        used = lens[base + b]
        row0 = pl.multiple_of(lax.rem(z - b + 4, 4) * HALF, HALF)
        offset = pl.multiple_of(offset, 16)
        offs[b] = offset
        first_mine = mine[pl.ds(row0, 16), :128].astype(F32)[:1]
        first_sib = sib[pl.ds(row0, 16), :128].astype(F32)[:1]
        filler = jnp.where(core == 0, first_mine, first_sib)
        for rel, source in enumerate((mine, sib)):
            side = core if rel == 0 else 1 - core
            for g in range(2):
                slot = g * 512 + side * 256
                rows = pl.ds(row0 + g * 256, 256)
                at = pl.ds(pl.multiple_of(offset + slot, 16), 256)

                @pl.when(slot + 256 <= used)
                def _():
                    ks[at, :] = source[rows, :128]
                    vs[at, :128] = source[rows, 128:]
                    vs[at, 128:] = jnp.ones((256, 128), BF)

                @pl.when((slot < used) & (slot + 256 > used))
                def _():
                    live = slot + lax.broadcasted_iota(jnp.int32, (256, 128), 0) < used
                    keys = source[rows, :128].astype(F32)
                    values = source[rows, 128:].astype(F32)
                    ks[at, :] = jnp.where(live, keys, filler).astype(BF)
                    vs[at, :128] = jnp.where(live, values, 0.0).astype(BF)
                    vs[at, 128:] = jnp.where(live, 1.0, 0.0).astype(BF)

        return offset + (used + 15) // 16 * 16

    end = lax.fori_loop(0, 4, block, 0)
    vs[pl.ds(pl.multiple_of(end, 16), KT), :] = jnp.zeros((KT, 256), BF)
    return end


def fold_tile(q, ks, vs, t, m_ref, acc_ref, i, limit_of):
    start = pl.multiple_of(t * KT, KT)
    keys = ks[pl.ds(start, KT), :]
    values = vs[pl.ds(start, KT), :]
    scores = [
        lax.dot_general(a, keys, (((1,), (1,)), ((), ())), preferred_element_type=F32) for a in q
    ]
    for g, s in enumerate(scores):
        if limit_of is not None:
            key = lax.broadcasted_iota(jnp.int32, (QT, KT), 1)
            s = jnp.where(key < limit_of(g) - start, s, NEGATIVE)
        rows = slice(g * QT, (g + 1) * QT)
        old = m_ref[i, rows]
        new = jnp.maximum(old, jnp.broadcast_to(jnp.max(s, axis=1, keepdims=True), (QT, 128)))
        p = jnp.exp2(s - wide(new, KT // 128)).astype(BF)
        acc_ref[i, rows] = acc_ref[i, rows] * wide(jnp.exp2(old - new), 2) + jnp.dot(
            p, values, preferred_element_type=F32
        )
        m_ref[i, rows] = new


def used_tiles(idx, lens, rel, body):
    block = lax.rem(idx[1] - rel + 4, 4)
    used = lens[idx[4] * 4 + block]
    firsts = [g * 512 + idx[0] * 256 for g in range(2)]

    @pl.when(firsts[1] < used)
    def _():
        body(2, block, used, firsts)

    @pl.when((firsts[1] >= used) & (firsts[0] < used))
    def _():
        body(1, block, used, firsts)


def attend_own_kernel(idx, lens, q0, q1, q2, q3, mine, sib, acc_ref, m_ref, ks, vs, offs):
    place_keys(idx, lens, idx[4] * 4, mine, sib, ks, vs, offs)
    for i, queries in enumerate((q0, q1, q2, q3)):

        def body(count, block, used, firsts):
            offset = offs[block]
            q = [queries[g * QT : (g + 1) * QT, :128] for g in range(count)]
            rows = slice(0, count * QT)
            m_ref[i, rows] = jnp.full((count * QT, 128), NEGATIVE, F32)
            acc_ref[i, rows] = jnp.zeros((count * QT, 256), F32)

            def limit_of(g):
                return offset + firsts[g] + 1 + lax.broadcasted_iota(jnp.int32, (QT, KT), 0)

            limit = offset + jnp.minimum(firsts[count - 1] + QT, used)
            whole = (offset + firsts[0] + 1) // KT
            tiles = (limit + KT - 1) // KT
            fold = functools.partial(fold_tile, q, ks, vs)
            lax.fori_loop(0, whole, lambda t, _: fold(t, m_ref, acc_ref, i, None), None)
            lax.fori_loop(whole, tiles, lambda t, _: fold(t, m_ref, acc_ref, i, limit_of), None)

        used_tiles(idx, lens, i, body)


def attend_own(idx, lens, pieces, mine, sib):
    return pl.pallas_call(
        attend_own_kernel,
        out_shape=(
            jax.ShapeDtypeStruct((4, HALF, 256), F32),
            jax.ShapeDtypeStruct((4, HALF, 128), F32),
        ),
        in_specs=[smem_spec()] * 2 + [vmem_spec()] * 6,
        out_specs=(vmem_spec(), vmem_spec()),
        scratch_shapes=[
            pltpu.VMEM((PACKED, 128), BF),
            pltpu.VMEM((PACKED, 256), BF),
            pltpu.SMEM((4,), jnp.int32),
        ],
        compiler_params=pltpu.CompilerParams(vmem_limit_bytes=24 * MIB),
        cost_estimate=pl.CostEstimate(
            flops=4 * CH * CH * 512, bytes_accessed=4 * MIB, transcendentals=4 * CH * CH
        ),
        name="attend_own",
    )(idx, lens, *pieces, mine, sib)


def attend_cross_kernel(
    which, idx, lens, q0, q1, mine, sib, acc_in, m_in, o_ref, ks, vs, offs, m_ref, acc_ref
):
    @pl.when(idx[4] == 1)
    def _():
        offs[4] = place_keys(idx, lens, 0, mine, sib, ks, vs, offs)

    o_ref[...] = jnp.zeros((2, HALF, 128), BF)
    for i, queries in enumerate((q0, q1)):

        def body(count, block, used, firsts):
            rows = slice(0, count * QT)
            acc_ref[0, rows] = acc_in[which[i], rows]

            @pl.when(idx[4] == 1)
            def _():
                end = offs[4]
                q = [queries[g * QT : (g + 1) * QT, :128] for g in range(count)]
                m_ref[0, rows] = m_in[which[i], rows]
                fold = functools.partial(fold_tile, q, ks, vs)
                whole = end // KT
                lax.fori_loop(0, whole, lambda t, _: fold(t, m_ref, acc_ref, 0, None), None)

                @pl.when(whole * KT < end)
                def _():
                    fold(whole, m_ref, acc_ref, 0, lambda g: end)

            for g in range(count):
                rows_g = slice(g * QT, (g + 1) * QT)
                row = firsts[g] + lax.broadcasted_iota(jnp.int32, (QT, 128), 0)
                out = acc_ref[0, rows_g, :128] / acc_ref[0, rows_g, 128:]
                o_ref[i, rows_g, :] = jnp.where(row < used, out, 0.0).astype(BF)

        used_tiles(idx, lens, which[i], body)


def attend_cross(which, idx, lens, pieces, mine, sib, state):
    return pl.pallas_call(
        functools.partial(attend_cross_kernel, which),
        out_shape=jax.ShapeDtypeStruct((2, HALF, 128), BF),
        in_specs=[smem_spec()] * 2 + [vmem_spec()] * 6,
        out_specs=vmem_spec(),
        scratch_shapes=[
            pltpu.VMEM((PACKED, 128), BF),
            pltpu.VMEM((PACKED, 256), BF),
            pltpu.SMEM((5,), jnp.int32),
            pltpu.VMEM((1, HALF, 128), F32),
            pltpu.VMEM((1, HALF, 256), F32),
        ],
        compiler_params=pltpu.CompilerParams(vmem_limit_bytes=24 * MIB),
        cost_estimate=pl.CostEstimate(
            flops=4 * CH * CH * 512, bytes_accessed=4 * MIB, transcendentals=4 * CH * CH
        ),
        name="attend_cross",
    )(idx, lens, *pieces, mine, sib, *state)


def decode_kernel(idx, lens, q_ref, keys, values, ok_ref, own, sib, out_ref, kc, vc, sems):
    core, me = idx[0], idx[5]
    used = lens[me]
    homes = [
        (idx[4] if n < 4 else 1 - idx[4]) * 4 + lax.rem(idx[1] - n % 4 + 4, 4) for n in range(8)
    ]
    loads = []
    for n in range(8):
        rows = pl.ds(pl.multiple_of(homes[n] * 16, 16), 16)
        loads.append(pltpu.make_async_copy(keys.at[rows], kc.at[n], sems.at[2 * n]))
        loads.append(pltpu.make_async_copy(values.at[rows], vc.at[n], sems.at[2 * n + 1]))
    for load in loads:
        load.start()
    nt = (((1,), (1,)), ((), ()))
    at = lax.broadcasted_iota(jnp.int32, (256, HALF), 1)
    slot = (at // 256) * 512 + at % 256
    ok_own = slot + core * 256 < used
    ok_sib = slot + (1 - core) * 256 < used
    prefix = []
    for head in range(2):
        cols = slice(head * 128, (head + 1) * 128)
        kcols = slice(256 + head * 128, 256 + (head + 1) * 128)
        vcols = slice(512 + head * 128, 512 + (head + 1) * 128)
        q = q_ref[:, cols]
        s_o = lax.dot_general(q, own[:HALF, kcols], nt, preferred_element_type=F32)
        s_s = lax.dot_general(q, sib[:HALF, kcols], nt, preferred_element_type=F32)
        s_o = jnp.where(ok_own, s_o, NEGATIVE)
        s_s = jnp.where(ok_sib, s_s, NEGATIVE)
        top = jnp.maximum(
            jnp.max(s_o, axis=1, keepdims=True), jnp.max(s_s, axis=1, keepdims=True)
        )
        p_o = jnp.exp2(s_o - top)
        p_s = jnp.exp2(s_s - top)
        total = jnp.sum(p_o, axis=1, keepdims=True) + jnp.sum(p_s, axis=1, keepdims=True)
        out = jnp.dot(p_o.astype(BF), own[:HALF, vcols], preferred_element_type=F32) + jnp.dot(
            p_s.astype(BF), sib[:HALF, vcols], preferred_element_type=F32
        )
        prefix.append((top, total, out))
    row = lax.broadcasted_iota(jnp.int32, (32, CH), 0)
    key = lax.broadcasted_iota(jnp.int32, (32, CH), 1)
    same = (row // 16) * 8 + row % 8 == key // 64
    lane = lax.broadcasted_iota(jnp.int32, (32, 128), 1)
    for n in range(8):
        loads[2 * n].wait()
        loads[2 * n + 1].wait()
        keys_c = kc[n].reshape(CH, 256)
        values_c = vc[n].reshape(CH, 256)
        ok = same & (ok_ref[pl.ds(homes[n], 1), :] > 0)
        rows = slice(n * 32, (n + 1) * 32)
        stats = []
        for head in range(2):
            cols = slice(head * 128, (head + 1) * 128)
            top, total, out = [a[rows] for a in prefix[head]]
            s = lax.dot_general(
                q_ref[rows, cols], keys_c[:, cols], nt, preferred_element_type=F32
            )
            s = jnp.where(ok, s, NEGATIVE)
            new = jnp.maximum(top, jnp.max(s, axis=1, keepdims=True))
            p = jnp.exp2(s - new)
            factor = jnp.exp2(top - new)
            stats += [new, factor * total + jnp.sum(p, axis=1, keepdims=True)]
            out_ref[n, :, cols] = factor * out + jnp.dot(
                p.astype(BF), values_c[:, cols], preferred_element_type=F32
            )
        out_ref[n, :, 256:] = jnp.where(
            lane < 32,
            stats[0],
            jnp.where(lane < 64, stats[1], jnp.where(lane < 96, stats[2], stats[3])),
        )


def decode_parts(idx, lens, queries, cache_keys, cache_values, ok, own, sib):
    hbm = pl.BlockSpec(memory_space=pltpu.HBM)
    return pl.pallas_call(
        decode_kernel,
        out_shape=jax.ShapeDtypeStruct((8, 32, 384), F32),
        in_specs=[smem_spec()] * 2 + [vmem_spec(), hbm, hbm] + [vmem_spec()] * 3,
        out_specs=vmem_spec(),
        scratch_shapes=[
            pltpu.VMEM((8, 16, 4, PANEL, 256), BF),
            pltpu.VMEM((8, 16, 4, PANEL, 256), BF),
            pltpu.SemaphoreType.DMA((16,)),
        ],
        compiler_params=pltpu.CompilerParams(vmem_limit_bytes=56 * MIB),
        cost_estimate=pl.CostEstimate(
            flops=8 * 32 * 2048 * 1024, bytes_accessed=10 * MIB, transcendentals=8 * 64 * 2048
        ),
        name="decode_parts",
    )(idx, lens, queries, cache_keys, cache_values, ok, own, sib)


def merge_kernel(parts, qkv_rows, out_ref):
    for head in range(2):
        cols = slice(head * 128, (head + 1) * 128)
        tops = [parts[n, :, 256 + head * 64 : 256 + head * 64 + 1] for n in range(8)]
        sums = [parts[n, :, 288 + head * 64 : 288 + head * 64 + 1] for n in range(8)]
        for side in range(2):
            for s in range(2):
                rows = slice(side * 16 + s * 8, side * 16 + s * 8 + 8)
                q = qkv_rows[rows, cols].astype(F32)
                fresh = []
                for u in range(s + 1):
                    from_rows = slice(side * 16 + u * 8, side * 16 + u * 8 + 8)
                    k = qkv_rows[from_rows, 256 + head * 128 : 384 + head * 128].astype(F32)
                    v = qkv_rows[from_rows, 512 + head * 128 : 640 + head * 128].astype(F32)
                    fresh.append((jnp.sum(q * k, axis=1, keepdims=True), v))
                top = fresh[0][0]
                for score, _ in fresh[1:]:
                    top = jnp.maximum(top, score)
                for part in tops:
                    top = jnp.maximum(top, part[rows])
                total = jnp.zeros((8, 1), F32)
                out = jnp.zeros((8, 128), F32)
                for score, v in fresh:
                    w = jnp.exp2(score - top)
                    total += w
                    out += w.astype(BF).astype(F32) * v
                for n in range(8):
                    w = jnp.exp2(tops[n][rows] - top)
                    total += w * sums[n][rows]
                    out += w * parts[n, rows, cols]
                out_ref[rows, cols] = (out / total).astype(BF)


def merge_parts(parts, qkv_rows):
    return pl.pallas_call(
        merge_kernel,
        out_shape=jax.ShapeDtypeStruct((32, 256), BF),
        in_specs=[vmem_spec()] * 2,
        out_specs=vmem_spec(),
        cost_estimate=pl.CostEstimate(flops=MIB, bytes_accessed=MIB, transcendentals=1000),
        name="merge_parts",
    )(parts, qkv_rows)


def head_order_kernel(idx, a, b, c, d, near, far, out_ref):
    for k, piece in enumerate((a, b, c, d)):
        column = pl.multiple_of(lax.rem(idx[1] + k - 2 * idx[0] + 4, 4) * 128, 128)
        out_ref[:HALF, pl.ds(column, 128)] = piece[...]
    out_ref[HALF:, :256] = near[...]
    out_ref[HALF:, 256:] = far[...]


def head_order(idx, pieces, near, far):
    return pl.pallas_call(
        head_order_kernel,
        out_shape=jax.ShapeDtypeStruct((ROWS, 512), BF),
        in_specs=[smem_spec()] + [vmem_spec()] * 6,
        out_specs=vmem_spec(),
        cost_estimate=pl.CostEstimate(flops=0, bytes_accessed=MIB, transcendentals=0),
        name="head_order",
    )(idx, *pieces, near, far)


def out_kernel(step, idx, *refs):
    chips, parts = STEPS_OF[step]
    count = (4, 3, 2)[step]
    pieces, ws, refs = refs[:count], refs[count : count + 4], refs[count + 4 :]
    totals, refs = (refs[:2], refs[2:]) if step else (None, refs)
    results, xs = refs[:2], refs[2]
    for n, row, place, start, size in parts:
        xs[start : start + size, place * 512 : (place + 1) * 512] = pieces[n][row : row + size, :]
    for rel in range(2):
        side = idx[0] if rel == 0 else 1 - idx[0]
        columns = pl.ds(pl.multiple_of(side * 256, 256), 256)
        result = None if totals is None else totals[rel][...]
        for place, (dx, dy) in enumerate(chips):
            k = -dy % 4
            for half, w in enumerate(ws[2 * dx : 2 * dx + 2]):
                at = place * 512 + half * 256
                term = jnp.dot(
                    xs[:, at : at + 256],
                    w[k * 256 : (k + 1) * 256, columns],
                    preferred_element_type=F32,
                )
                result = term if result is None else result + term
        results[rel][...] = result


def out_project(step, idx, pieces, weights, totals=()):
    chips = len(STEPS_OF[step][0])
    return pl.pallas_call(
        functools.partial(out_kernel, step),
        out_shape=(
            jax.ShapeDtypeStruct((ROWS, 256), F32),
            jax.ShapeDtypeStruct((ROWS, 256), F32),
        ),
        in_specs=[smem_spec()] + [vmem_spec()] * (len(pieces) + 4 + len(totals)),
        out_specs=(vmem_spec(), vmem_spec()),
        scratch_shapes=[pltpu.VMEM((ROWS, chips * 512), BF)],
        compiler_params=pltpu.CompilerParams(vmem_limit_bytes=20 * MIB),
        cost_estimate=pl.CostEstimate(
            flops=2 * ROWS * 512 * chips * 512, bytes_accessed=4 * MIB, transcendentals=0
        ),
        name="out_project",
    )(idx, *pieces, *weights, *totals)


def pick(pair, core):
    return jnp.where(core == 0, pair[0], pair[1])


def shards(
    prompt,
    decode_tokens,
    query_weight,
    key_weight,
    value_weight,
    out_weight,
    cache_keys,
    cache_values,
    stretch_lengths,
    panel_map,
    ctx_lengths,
):
    inst = lax.axis_index("inst")
    tp = lax.axis_index("tp")
    core = tp % 2
    y = (tp // 2) % 4
    x = tp // 8
    z = inst % 4
    xh = inst // 4
    idx = jnp.stack([core, z, x, y, xh, inst, 0, 0]).astype(jnp.int32)

    groups = prompt.reshape(2, 2, GROUP, 256)
    tokens = decode_tokens.reshape(STEPS, 2, 8, 256)
    halves = [
        jnp.concatenate(
            [groups[:, n].reshape(HALF, 256), tokens[:, n].reshape(DEC, 256)], axis=0
        )
        for n in range(2)
    ]
    mine, theirs = pick(halves, core), pick(halves[::-1], core)
    received = move(theirs, dc=1)
    query_w, key_w, received = lax.optimization_barrier((query_weight, key_weight, received))
    first = gather_first(jnp.concatenate([mine, received], axis=1))
    sib_query, sib_key = move(query_w, dc=1), move(key_w, dc=1)
    value_w, *rest = lax.optimization_barrier((value_weight, *first[1:]))
    first = (first[0], *rest)
    sib_value = move(value_w, dc=1)
    second = gather_second(first)
    weights = (query_weight, key_weight, value_weight, sib_query, sib_key, sib_value)
    total = qkv(0, idx, first, weights)
    total, *second = lax.optimization_barrier((total, *second))
    third = gather_third(second)
    total = qkv(1, idx, second, weights, (total,))
    by_owner, by_head = qkv(2, idx, third, weights, (total,))

    own = by_head[0]
    heads = [move(by_head[k], dz=k) for k in (1, 3, 2)]
    one, three, two, own, out_w, rows_out = lax.optimization_barrier(
        (*heads, own, out_weight, by_owner[1])
    )
    blocks = (own, one, two, three)
    queries = jnp.stack([a[HALF:, :256].reshape(2, DEC, 256) for a in blocks])
    other_queries = move(queries, dxh=1)
    mine = pack(blocks)
    other_queries, cross = lax.optimization_barrier((other_queries, mine))
    cross = move(cross, dxh=1, only_xh=0)
    sib = move(mine, dc=1)

    from_sib = move(rows_out, dc=1)
    own_rows = by_owner[0]
    pair = (own_rows[HALF:], from_sib[HALF:])
    dec_rows = jnp.concatenate([pick(pair, core), pick(pair[::-1], core)], axis=0)
    queries = jnp.concatenate([queries, other_queries], axis=0)
    pair = (queries[:, 0], move(queries[:, 1], dc=1))
    queries = jnp.concatenate([pick(pair, core), pick(pair[::-1], core)], axis=1)
    queries = queries.reshape(256, 256)

    spread = []
    for dy in range(4):
        at = (y + dy) % 4 * 512
        columns = jnp.concatenate(
            [
                lax.dynamic_slice_in_dim(out_w, side * 2048 + at, 512, axis=1)
                for side in (x, 1 - x)
            ],
            axis=1,
        )
        spread.append(columns if dy == 0 else move(columns, dy=dy))

    state = attend_own(idx, stretch_lengths, blocks, mine, sib)
    positions = (
        panel_map[:, :, None] * PANEL + jnp.arange(PANEL, dtype=jnp.int32)[None, None, :]
    )
    ok = (positions < ctx_lengths[:, None, None]).astype(F32).reshape(8, CH)
    parts = decode_parts(
        idx, stretch_lengths, queries, cache_keys, cache_values, ok, own_rows, from_sib
    )
    cross, parts, *rest = lax.optimization_barrier((cross, parts, *state, *spread))
    state, spread = rest[:2], rest[2:]
    cross_sib = move(cross, dc=1)
    moved = move(parts[4:], dxh=1)
    far = move(jnp.concatenate([w[:, 512:] for w in spread], axis=0), dxl=1)
    first_heads = attend_cross(
        (1, 2), idx, stretch_lengths, (one, two), cross, cross_sib, state
    )
    parts = jnp.stack([parts[:4], moved])
    parts, first_heads, cross = lax.optimization_barrier((parts, first_heads, cross))
    moved = [move(parts[:, k], dz=4 - k) for k in (1, 2, 3)]
    back_one = move(first_heads[0], dz=3)
    back_two = move(first_heads[1], dz=2)
    last_heads = attend_cross(
        (3, 0), idx, stretch_lengths, (three, own), cross, cross_sib, state
    )
    last_heads, far, *spread = lax.optimization_barrier((last_heads, far, *spread))
    near = jnp.concatenate([w[:, :512] for w in spread], axis=0)
    back_three = move(last_heads[0], dz=1)
    parts = jnp.stack([parts[:, 0], *moved], axis=1).reshape(8, 32, 384)
    dec_attn = merge_parts(parts, dec_rows)
    mine = pick((dec_attn[:DEC], dec_attn[DEC:]), core)
    theirs = move(pick((dec_attn[DEC:], dec_attn[:DEC]), core), dc=1)
    attn = head_order(idx, (last_heads[1], back_one, back_two, back_three), mine, theirs)
    first = gather_first(attn)
    attn, near, far = lax.optimization_barrier((attn, near, far))
    weights = (near, move(near, dc=1), far, move(far, dc=1))
    second = gather_second(first)
    totals = out_project(0, idx, first, weights)
    *totals, up, down, across = lax.optimization_barrier((*totals, *second))
    second = (up, down, across)
    third = gather_third(second)
    totals = out_project(1, idx, second, weights, totals)
    mine, theirs = out_project(2, idx, third, weights, totals)
    received = move(theirs, dc=1)
    pair = (mine, received)
    sides = [pick(pair, core), pick(pair[::-1], core)]
    prefill_out = jnp.stack(
        [side[:HALF].reshape(2, GROUP, 256) for side in sides], axis=1
    ).reshape(CH, 256)
    decode_out = jnp.stack(
        [side[HALF:].reshape(STEPS, 8, 256) for side in sides], axis=1
    ).reshape(STEPS, 16, 256)
    return prefill_out, decode_out


def solution(mesh):
    return jax.shard_map(
        shards,
        mesh=mesh,
        in_specs=(
            P("inst", "tp"),
            P(None, "inst", "tp"),
            P(None, "tp"),
            P(None, "tp"),
            P(None, "tp"),
            P("tp", None),
            P(None, "inst", None, "tp"),
            P(None, "inst", None, "tp"),
            P(),
            P(None, "inst"),
            P(),
        ),
        out_specs=(P("inst", "tp"), P(None, "inst", "tp")),
        check_vma=False,
    )
```

```python
import functools
import math

import jax
import jax.numpy as jnp
from jax import lax
from jax.experimental import pallas as pl
from jax.experimental.pallas import tpu as pltpu
from jax.sharding import PartitionSpec as P

HD = 128
CH = 1024
PANEL = 16
STEPS = 2
NEGATIVE = -1e30
SCALE = math.log2(math.e) / math.sqrt(HD)
AX = ("inst", "tp")
HALF = 512
GROUP = 256
DEC = 16
ROWS = HALF + DEC
CUT = 256
BF = jnp.bfloat16
F32 = jnp.float32
MIB = 1 << 20


def perm(dxh=0, dz=0, dxl=0, dy=0, dc=0, only_xh=None, zxor=0):
    pairs = []
    for xh in range(2):
        if only_xh is not None and xh != only_xh:
            continue
        for z in range(4):
            for xl in range(2):
                for y in range(4):
                    for c in range(2):
                        source = (xh * 4 + z) * 16 + xl * 8 + y * 2 + c
                        target = (
                            ((xh ^ dxh) * 4 + (((z + dz) % 4) ^ zxor)) * 16
                            + (xl ^ dxl) * 8
                            + ((y + dy) % 4) * 2
                            + (c ^ dc)
                        )
                        pairs.append((source, target))
    return pairs


def move(x, **steps):
    return lax.ppermute(x, AX, perm(**steps))


LOW = slice(0, CUT)
HIGH = ROWS - CUT


def gather_first(own):
    return own, move(own, dy=1), move(own, dy=-1), move(own, dxl=1)


def gather_second(first):
    _, before, after, beside = first
    up = move(jnp.concatenate([before[LOW], beside[CUT:]]), dy=1)
    down = move(jnp.concatenate([after[CUT:], beside[CUT:]]), dy=-1)
    across = move(jnp.concatenate([before[LOW], after[LOW]]), dxl=1)
    return up, down, across


def gather_third(second):
    _, down, across = second
    return move(across[LOW], dy=1), move(down[HIGH:], dy=-1)


STEPS_OF = (
    (
        ((0, 0), (0, -1), (0, 1), (1, 0)),
        tuple((n, 0, n, 0, ROWS) for n in range(4)),
    ),
    (
        ((0, 2), (1, -1), (1, 1)),
        (
            (0, 0, 0, 0, CUT), (0, CUT, 1, CUT, HIGH),
            (1, 0, 0, CUT, HIGH), (1, HIGH, 2, CUT, HIGH),
            (2, 0, 1, 0, CUT), (2, CUT, 2, 0, CUT),
        ),
    ),
    (((1, 2),), ((0, 0, 0, 0, CUT), (1, 0, 0, CUT, HIGH))),
)


def chip_at(idx, dx, dy):
    x = idx[2]
    x = 1 - x if dx else x
    return x * 4 + lax.rem(idx[3] + dy + 4, 4)


def qkv_kernel(step, idx, *refs):
    chips, parts = STEPS_OF[step]
    count = (4, 3, 2)[step]
    pieces, weights, refs = refs[:count], refs[count : count + 6], refs[count + 6 :]
    total, refs = (refs[0], refs[1:]) if step else (None, refs)
    xs, ws, sems = refs[-3:]
    core, z = idx[0], idx[1]
    copies = []
    for n in range(6):
        for place, (dx, dy) in enumerate(chips):
            rows = pl.ds(pl.multiple_of(chip_at(idx, dx, dy) * 512, 512), 512)
            copies.append(
                pltpu.make_async_copy(
                    weights[n].at[rows, :],
                    ws.at[n, pl.ds(place * 512, 512), :],
                    sems.at[len(copies)],
                )
            )
    for copy in copies:
        copy.start()
    for n, row, place, start, size in parts:
        for half in range(2):
            side = core if half == 0 else 1 - core
            column = pl.multiple_of(place * 512 + side * 256, 256)
            xs[start : start + size, pl.ds(column, 256)] = pieces[n][
                row : row + size, half * 256 : (half + 1) * 256
            ]

    def product(n):
        for place in range(len(chips)):
            pltpu.make_async_copy(
                weights[0].at[pl.ds(0, 512), :],
                ws.at[n, pl.ds(place * 512, 512), :],
                sems.at[n * len(chips) + place],
            ).wait()
        result = jnp.dot(xs[...], ws[n], preferred_element_type=F32)
        return result if total is None else result + total[n]

    if step < 2:

        def one(n, _):
            refs[0][n] = product(n)

        lax.fori_loop(0, 6, one, None)
        return
    for n in range(6):
        result = product(n)
        y_ref, z_refs = refs[0], refs[1:5]
        rel, kind = n // 3, n % 3
        owner = core if rel == 0 else 1 - core
        if kind == 0:
            result = result * SCALE
        result = result.astype(BF)
        for head in range(2):
            slot = lax.rem(owner * 2 + head - z + 4, 4)
            for k in range(4):

                @pl.when(slot == k)
                def _():
                    z_refs[k][:HALF, kind * 128 : (kind + 1) * 128] = result[
                        :HALF, head * 128 : (head + 1) * 128
                    ]

        if kind == 0:
            rows = slice(HALF + rel * DEC, HALF + (rel + 1) * DEC)
            for z_ref in z_refs:
                z_ref[rows, :256] = result[HALF:]
                z_ref[rows, 256:] = result[HALF:, :128]
        if rel == 1:
            refs[5][:, kind * 256 : (kind + 1) * 256] = result
        else:
            y_ref[:, kind * 256 : (kind + 1) * 256] = result


def vmem_spec():
    return pl.BlockSpec(memory_space=pltpu.VMEM)


def smem_spec():
    return pl.BlockSpec(memory_space=pltpu.SMEM)


def qkv(step, idx, pieces, weights, total=()):
    chips = len(STEPS_OF[step][0])
    shape = jax.ShapeDtypeStruct((6, ROWS, 256), F32)
    if step == 2:
        shape = (
            jax.ShapeDtypeStruct((ROWS, 768), BF),
            *[jax.ShapeDtypeStruct((HALF + 2 * DEC, 384), BF)] * 4,
            jax.ShapeDtypeStruct((ROWS, 768), BF),
        )
    return pl.pallas_call(
        functools.partial(qkv_kernel, step),
        out_shape=shape,
        in_specs=[smem_spec()]
        + [vmem_spec()] * len(pieces)
        + [pl.BlockSpec(memory_space=pltpu.HBM)] * 6
        + [vmem_spec()] * len(total),
        out_specs=(vmem_spec(),) * 6 if step == 2 else vmem_spec(),
        scratch_shapes=[
            pltpu.VMEM((ROWS, chips * 512), BF),
            pltpu.VMEM((6, chips * 512, 256), BF),
            pltpu.SemaphoreType.DMA((6 * chips,)),
        ],
        compiler_params=pltpu.CompilerParams(vmem_limit_bytes=(56, 40, 18)[step] * MIB),
        cost_estimate=pl.CostEstimate(
            flops=2 * ROWS * 512 * chips * 1536, bytes_accessed=8 * MIB, transcendentals=0
        ),
        name="qkv",
    )(idx, *pieces, *weights, *total)


def pack_kernel(a, b, c, d, out_ref):
    for n, piece in enumerate((a, b, c, d)):
        out_ref[n * HALF : (n + 1) * HALF, :] = piece[:HALF, 128:]


def pack(pieces):
    return pl.pallas_call(
        pack_kernel,
        out_shape=jax.ShapeDtypeStruct((4 * HALF, 256), BF),
        in_specs=[vmem_spec()] * 4,
        out_specs=vmem_spec(),
        compiler_params=pltpu.CompilerParams(vmem_limit_bytes=8 * MIB),
        cost_estimate=pl.CostEstimate(flops=0, bytes_accessed=4 * MIB, transcendentals=0),
        name="pack",
    )(*pieces)


def pack_weight_kernel(a, b, c, d, near_ref, far_ref):
    for n, piece in enumerate((a, b, c, d)):
        near_ref[n * 256 : (n + 1) * 256, :] = piece[:, :512]
        far_ref[n * 256 : (n + 1) * 256, :] = piece[:, 512:]


def pack_weight(pieces):
    return pl.pallas_call(
        pack_weight_kernel,
        out_shape=(jax.ShapeDtypeStruct((1024, 512), BF),) * 2,
        in_specs=[vmem_spec()] * 4,
        out_specs=(vmem_spec(),) * 2,
        compiler_params=pltpu.CompilerParams(vmem_limit_bytes=8 * MIB),
        cost_estimate=pl.CostEstimate(flops=0, bytes_accessed=4 * MIB, transcendentals=0),
        name="pack_weight",
    )(*pieces)


QT = 256
KT = 1024
PACKED = 5 * CH + 256


def wide(a, n):
    return jnp.concatenate([a] * n, axis=1)


def place_keys(idx, lens, base, mine, sib, ks, vs, offs):
    core, z = idx[0], idx[1]

    def block(b, offset):
        used = lens[base + b]
        row0 = pl.multiple_of(lax.rem(z - b + 4, 4) * HALF, HALF)
        offset = pl.multiple_of(offset, 16)
        offs[b] = offset
        first_mine = mine[pl.ds(row0, 16), :128].astype(F32)[:1]
        first_sib = sib[pl.ds(row0, 16), :128].astype(F32)[:1]
        filler = jnp.where(core == 0, first_mine, first_sib)
        for rel, source in enumerate((mine, sib)):
            side = core if rel == 0 else 1 - core
            for g in range(2):
                slot = g * 512 + side * 256
                rows = pl.ds(row0 + g * 256, 256)
                at = pl.ds(pl.multiple_of(offset + slot, 16), 256)

                @pl.when(slot + 256 <= used)
                def _():
                    ks[at, :] = source[rows, :128]
                    vs[at, :128] = source[rows, 128:]
                    vs[at, 128:] = jnp.ones((256, 128), BF)

                @pl.when((slot < used) & (slot + 256 > used))
                def _():
                    live = slot + lax.broadcasted_iota(jnp.int32, (256, 128), 0) < used
                    keys = source[rows, :128].astype(F32)
                    values = source[rows, 128:].astype(F32)
                    ks[at, :] = jnp.where(live, keys, filler).astype(BF)
                    vs[at, :128] = jnp.where(live, values, 0.0).astype(BF)
                    vs[at, 128:] = jnp.where(live, 1.0, 0.0).astype(BF)

        return offset + (used + 15) // 16 * 16

    end = lax.fori_loop(0, 4, block, 0)
    vs[pl.ds(pl.multiple_of(end, 16), KT), :] = jnp.zeros((KT, 256), BF)
    return end


def fold_tile(q, ks, vs, t, m_ref, acc_ref, i, limit_of):
    start = pl.multiple_of(t * KT, KT)
    keys = ks[pl.ds(start, KT), :]
    values = vs[pl.ds(start, KT), :]
    scores = [
        lax.dot_general(a, keys, (((1,), (1,)), ((), ())), preferred_element_type=F32) for a in q
    ]
    for g, s in enumerate(scores):
        if limit_of is not None:
            key = lax.broadcasted_iota(jnp.int32, (QT, KT), 1)
            s = jnp.where(key < limit_of(g) - start, s, NEGATIVE)
        rows = slice(g * QT, (g + 1) * QT)
        old = m_ref[i, rows]
        new = jnp.maximum(old, jnp.broadcast_to(jnp.max(s, axis=1, keepdims=True), (QT, 128)))
        p = jnp.exp2(s - wide(new, KT // 128)).astype(BF)
        acc_ref[i, rows] = acc_ref[i, rows] * wide(jnp.exp2(old - new), 2) + jnp.dot(
            p, values, preferred_element_type=F32
        )
        m_ref[i, rows] = new


def used_blocks(idx, lens, first, count, body):
    def one(i, _):
        block = lax.rem(idx[1] - first - i + 4, 4)
        used = lens[idx[4] * 4 + block]

        @pl.when(idx[0] * 256 < used)
        def _():
            body(i, block, used)

    lax.fori_loop(0, count, one, None)


def attend_own_kernel(idx, lens, q0, q1, q2, q3, mine, sib, acc_ref, m_ref, qs, ks, vs, offs):
    place_keys(idx, lens, idx[4] * 4, mine, sib, ks, vs, offs)
    for i, queries in enumerate((q0, q1, q2, q3)):
        qs[i] = queries[:HALF, :128]
    firsts = [g * 512 + idx[0] * 256 for g in range(2)]

    def body(i, block, used):
        offset = offs[block]
        q = [qs[i, g * QT : (g + 1) * QT, :] for g in range(2)]
        m_ref[i] = jnp.full((HALF, 128), NEGATIVE, F32)
        acc_ref[i] = jnp.zeros((HALF, 256), F32)

        def limit_of(g):
            return offset + firsts[g] + 1 + lax.broadcasted_iota(jnp.int32, (QT, KT), 0)

        limit = offset + jnp.minimum(firsts[1] + QT, used)
        whole = (offset + firsts[0] + 1) // KT
        tiles = (limit + KT - 1) // KT
        fold = functools.partial(fold_tile, q, ks, vs)
        lax.fori_loop(0, whole, lambda t, _: fold(t, m_ref, acc_ref, i, None), None)
        lax.fori_loop(whole, tiles, lambda t, _: fold(t, m_ref, acc_ref, i, limit_of), None)

    used_blocks(idx, lens, 0, 4, body)


def attend_own(idx, lens, pieces, mine, sib):
    return pl.pallas_call(
        attend_own_kernel,
        out_shape=(
            jax.ShapeDtypeStruct((4, HALF, 256), F32),
            jax.ShapeDtypeStruct((4, HALF, 128), F32),
        ),
        in_specs=[smem_spec()] * 2 + [vmem_spec()] * 6,
        out_specs=(vmem_spec(), vmem_spec()),
        scratch_shapes=[
            pltpu.VMEM((4, HALF, 128), BF),
            pltpu.VMEM((PACKED, 128), BF),
            pltpu.VMEM((PACKED, 256), BF),
            pltpu.SMEM((4,), jnp.int32),
        ],
        compiler_params=pltpu.CompilerParams(vmem_limit_bytes=24 * MIB),
        cost_estimate=pl.CostEstimate(
            flops=4 * CH * CH * 512, bytes_accessed=4 * MIB, transcendentals=4 * CH * CH
        ),
        name="attend_own",
    )(idx, lens, *pieces, mine, sib)


def attend_cross_kernel(which, idx, lens, *refs):
    count = len(which)
    pieces = refs[:count]
    mine, sib, acc_in, m_in, o_ref, qs, ks, vs, offs, m_ref, acc_ref = refs[count:]

    @pl.when(idx[4] == 1)
    def _():
        offs[4] = place_keys(idx, lens, 0, mine, sib, ks, vs, offs)

    o_ref[...] = jnp.zeros((count, HALF, 128), BF)
    for i, queries in enumerate(pieces):
        qs[i] = queries[:HALF, :128]

    def body(i, block, used):
        acc_ref[0] = acc_in[which[0] + i]

        @pl.when(idx[4] == 1)
        def _():
            end = offs[4]
            q = [qs[i, g * QT : (g + 1) * QT, :] for g in range(2)]
            m_ref[0] = m_in[which[0] + i]
            fold = functools.partial(fold_tile, q, ks, vs)
            whole = end // KT
            lax.fori_loop(0, whole, lambda t, _: fold(t, m_ref, acc_ref, 0, None), None)

            @pl.when(whole * KT < end)
            def _():
                fold(whole, m_ref, acc_ref, 0, lambda g: end)

        for g in range(2):
            rows = slice(g * QT, (g + 1) * QT)
            row = g * 512 + idx[0] * 256 + lax.broadcasted_iota(jnp.int32, (QT, 128), 0)
            out = acc_ref[0, rows, :128] / acc_ref[0, rows, 128:]
            o_ref[i, rows, :] = jnp.where(row < used, out, 0.0).astype(BF)

    used_blocks(idx, lens, which[0], count, body)


def attend_cross(which, idx, lens, pieces, mine, sib, state):
    return pl.pallas_call(
        functools.partial(attend_cross_kernel, which),
        out_shape=jax.ShapeDtypeStruct((len(which), HALF, 128), BF),
        in_specs=[smem_spec()] * 2 + [vmem_spec()] * (len(which) + 4),
        out_specs=vmem_spec(),
        scratch_shapes=[
            pltpu.VMEM((len(which), HALF, 128), BF),
            pltpu.VMEM((PACKED, 128), BF),
            pltpu.VMEM((PACKED, 256), BF),
            pltpu.SMEM((5,), jnp.int32),
            pltpu.VMEM((1, HALF, 128), F32),
            pltpu.VMEM((1, HALF, 256), F32),
        ],
        compiler_params=pltpu.CompilerParams(vmem_limit_bytes=24 * MIB),
        cost_estimate=pl.CostEstimate(
            flops=4 * CH * CH * 512, bytes_accessed=4 * MIB, transcendentals=4 * CH * CH
        ),
        name="attend_cross",
    )(idx, lens, *pieces, mine, sib, *state)


def decode_kernel(idx, lens, q_ref, keys, values, ok_ref, own, sib, out_ref, kc, vc, tops, sums, outs, sems):
    core, me = idx[0], idx[5]
    used = lens[me]

    def loads(n):
        home = (idx[4] ^ (n // 4)) * 4 + lax.rem(idx[1] - lax.rem(n, 4) + 4, 4)
        rows = pl.ds(pl.multiple_of(home * 16, 16), 16)
        return home, (
            pltpu.make_async_copy(keys.at[rows], kc.at[n], sems.at[2 * n]),
            pltpu.make_async_copy(values.at[rows], vc.at[n], sems.at[2 * n + 1]),
        )

    for n in range(8):
        for load in loads(n)[1]:
            load.start()
    nt = (((1,), (1,)), ((), ()))
    at = lax.broadcasted_iota(jnp.int32, (256, HALF), 1)
    slot = (at // 256) * 512 + at % 256
    ok_own = slot + core * 256 < used
    ok_sib = slot + (1 - core) * 256 < used
    for head in range(2):
        cols = slice(head * 128, (head + 1) * 128)
        kcols = slice(256 + head * 128, 256 + (head + 1) * 128)
        vcols = slice(512 + head * 128, 512 + (head + 1) * 128)
        q = q_ref[:, cols]
        s_o = lax.dot_general(q, own[:HALF, kcols], nt, preferred_element_type=F32)
        s_s = lax.dot_general(q, sib[:HALF, kcols], nt, preferred_element_type=F32)
        s_o = jnp.where(ok_own, s_o, NEGATIVE)
        s_s = jnp.where(ok_sib, s_s, NEGATIVE)
        top = jnp.maximum(
            jnp.max(s_o, axis=1, keepdims=True), jnp.max(s_s, axis=1, keepdims=True)
        )
        p_o = jnp.exp2(s_o - top)
        p_s = jnp.exp2(s_s - top)
        total = jnp.sum(p_o, axis=1, keepdims=True) + jnp.sum(p_s, axis=1, keepdims=True)
        out = jnp.dot(p_o.astype(BF), own[:HALF, vcols], preferred_element_type=F32) + jnp.dot(
            p_s.astype(BF), sib[:HALF, vcols], preferred_element_type=F32
        )
        tops[head] = jnp.broadcast_to(top, (256, 128))
        sums[head] = jnp.broadcast_to(total, (256, 128))
        outs[head] = out
    row = lax.broadcasted_iota(jnp.int32, (32, CH), 0)
    key = lax.broadcasted_iota(jnp.int32, (32, CH), 1)
    same = (row // 16) * 8 + row % 8 == key // 64
    lane = lax.broadcasted_iota(jnp.int32, (32, 128), 1)

    def group(n, _):
        home, copies = loads(n)
        for copy in copies:
            copy.wait()
        keys_c = kc[n].reshape(CH, 256)
        values_c = vc[n].reshape(CH, 256)
        ok = same & (ok_ref[pl.ds(home, 1), :] > 0)
        rows = pl.ds(pl.multiple_of(n * 32, 32), 32)
        stats = []
        for head in range(2):
            cols = slice(head * 128, (head + 1) * 128)
            top = tops[head, rows, :1]
            s = lax.dot_general(
                q_ref[rows, cols], keys_c[:, cols], nt, preferred_element_type=F32
            )
            s = jnp.where(ok, s, NEGATIVE)
            new = jnp.maximum(top, jnp.max(s, axis=1, keepdims=True))
            p = jnp.exp2(s - new)
            factor = jnp.exp2(top - new)
            stats += [new, factor * sums[head, rows, :1] + jnp.sum(p, axis=1, keepdims=True)]
            out_ref[n, :, cols] = factor * outs[head, rows, :] + jnp.dot(
                p.astype(BF), values_c[:, cols], preferred_element_type=F32
            )
        out_ref[n, :, 256:] = jnp.where(
            lane < 32,
            stats[0],
            jnp.where(lane < 64, stats[1], jnp.where(lane < 96, stats[2], stats[3])),
        )

    lax.fori_loop(0, 8, group, None)


def decode_parts(idx, lens, queries, cache_keys, cache_values, ok, own, sib):
    hbm = pl.BlockSpec(memory_space=pltpu.HBM)
    return pl.pallas_call(
        decode_kernel,
        out_shape=jax.ShapeDtypeStruct((8, 32, 384), F32),
        in_specs=[smem_spec()] * 2 + [vmem_spec(), hbm, hbm] + [vmem_spec()] * 3,
        out_specs=vmem_spec(),
        scratch_shapes=[
            pltpu.VMEM((8, 16, 4, PANEL, 256), BF),
            pltpu.VMEM((8, 16, 4, PANEL, 256), BF),
            *[pltpu.VMEM((2, 256, 128), F32)] * 3,
            pltpu.SemaphoreType.DMA((16,)),
        ],
        compiler_params=pltpu.CompilerParams(vmem_limit_bytes=50 * MIB),
        cost_estimate=pl.CostEstimate(
            flops=8 * 32 * 2048 * 1024, bytes_accessed=10 * MIB, transcendentals=8 * 64 * 2048
        ),
        name="decode_parts",
    )(idx, lens, queries, cache_keys, cache_values, ok, own, sib)


def merge_kernel(parts, qkv_rows, out_ref):
    for head in range(2):
        cols = slice(head * 128, (head + 1) * 128)
        tops = [parts[n, :, 256 + head * 64 : 256 + head * 64 + 1] for n in range(8)]
        sums = [parts[n, :, 288 + head * 64 : 288 + head * 64 + 1] for n in range(8)]
        for side in range(2):
            for s in range(2):
                rows = slice(side * 16 + s * 8, side * 16 + s * 8 + 8)
                q = qkv_rows[rows, cols].astype(F32)
                fresh = []
                for u in range(s + 1):
                    from_rows = slice(side * 16 + u * 8, side * 16 + u * 8 + 8)
                    k = qkv_rows[from_rows, 256 + head * 128 : 384 + head * 128].astype(F32)
                    v = qkv_rows[from_rows, 512 + head * 128 : 640 + head * 128].astype(F32)
                    fresh.append((jnp.sum(q * k, axis=1, keepdims=True), v))
                top = fresh[0][0]
                for score, _ in fresh[1:]:
                    top = jnp.maximum(top, score)
                for part in tops:
                    top = jnp.maximum(top, part[rows])
                total = jnp.zeros((8, 1), F32)
                out = jnp.zeros((8, 128), F32)
                for score, v in fresh:
                    w = jnp.exp2(score - top)
                    total += w
                    out += w.astype(BF).astype(F32) * v
                for n in range(8):
                    w = jnp.exp2(tops[n][rows] - top)
                    total += w * sums[n][rows]
                    out += w * parts[n, rows, cols]
                out_ref[rows, cols] = (out / total).astype(BF)


def merge_parts(parts, qkv_rows):
    return pl.pallas_call(
        merge_kernel,
        out_shape=jax.ShapeDtypeStruct((32, 256), BF),
        in_specs=[vmem_spec()] * 2,
        out_specs=vmem_spec(),
        compiler_params=pltpu.CompilerParams(vmem_limit_bytes=4 * MIB),
        cost_estimate=pl.CostEstimate(flops=MIB, bytes_accessed=MIB, transcendentals=1000),
        name="merge_parts",
    )(parts, qkv_rows)


def head_order_kernel(idx, a, b, c, d, near, far, out_ref):
    for k, piece in enumerate((a, b, c, d)):
        column = pl.multiple_of(lax.rem(idx[1] + k - 2 * idx[0] + 4, 4) * 128, 128)
        out_ref[:HALF, pl.ds(column, 128)] = piece[...]
    out_ref[HALF:, :256] = near[...]
    out_ref[HALF:, 256:] = far[...]


def head_order(idx, pieces, near, far):
    return pl.pallas_call(
        head_order_kernel,
        out_shape=jax.ShapeDtypeStruct((ROWS, 512), BF),
        in_specs=[smem_spec()] + [vmem_spec()] * 6,
        out_specs=vmem_spec(),
        compiler_params=pltpu.CompilerParams(vmem_limit_bytes=4 * MIB),
        cost_estimate=pl.CostEstimate(flops=0, bytes_accessed=MIB, transcendentals=0),
        name="head_order",
    )(idx, *pieces, near, far)


def out_kernel(step, idx, *refs):
    chips, parts = STEPS_OF[step]
    count = (4, 3, 2)[step]
    pieces, ws, refs = refs[:count], refs[count : count + 4], refs[count + 4 :]
    totals, refs = (refs[:2], refs[2:]) if step else (None, refs)
    results, xs = refs[:2], refs[2]
    for n, row, place, start, size in parts:
        xs[start : start + size, place * 512 : (place + 1) * 512] = pieces[n][row : row + size, :]
    for rel in range(2):
        side = idx[0] if rel == 0 else 1 - idx[0]
        columns = pl.ds(pl.multiple_of(side * 256, 256), 256)
        result = None if totals is None else totals[rel][...]
        for place, (dx, dy) in enumerate(chips):
            k = -dy % 4
            for half, w in enumerate(ws[2 * dx : 2 * dx + 2]):
                at = place * 512 + half * 256
                term = jnp.dot(
                    xs[:, at : at + 256],
                    w[k * 256 : (k + 1) * 256, columns],
                    preferred_element_type=F32,
                )
                result = term if result is None else result + term
        results[rel][...] = result


def out_project(step, idx, pieces, weights, totals=()):
    chips = len(STEPS_OF[step][0])
    return pl.pallas_call(
        functools.partial(out_kernel, step),
        out_shape=(
            jax.ShapeDtypeStruct((ROWS, 256), F32),
            jax.ShapeDtypeStruct((ROWS, 256), F32),
        ),
        in_specs=[smem_spec()] + [vmem_spec()] * (len(pieces) + 4 + len(totals)),
        out_specs=(vmem_spec(), vmem_spec()),
        scratch_shapes=[pltpu.VMEM((ROWS, chips * 512), BF)],
        compiler_params=pltpu.CompilerParams(vmem_limit_bytes=20 * MIB),
        cost_estimate=pl.CostEstimate(
            flops=2 * ROWS * 512 * chips * 512, bytes_accessed=4 * MIB, transcendentals=0
        ),
        name="out_project",
    )(idx, *pieces, *weights, *totals)


def pick(pair, core):
    return jnp.where(core == 0, pair[0], pair[1])


def shards(
    prompt,
    decode_tokens,
    query_weight,
    key_weight,
    value_weight,
    out_weight,
    cache_keys,
    cache_values,
    stretch_lengths,
    panel_map,
    ctx_lengths,
):
    inst = lax.axis_index("inst")
    tp = lax.axis_index("tp")
    core = tp % 2
    y = (tp // 2) % 4
    x = tp // 8
    z = inst % 4
    xh = inst // 4
    idx = jnp.stack([core, z, x, y, xh, inst, 0, 0]).astype(jnp.int32)

    groups = prompt.reshape(2, 2, GROUP, 256)
    tokens = decode_tokens.reshape(STEPS, 2, 8, 256)
    halves = [
        jnp.concatenate(
            [groups[:, n].reshape(HALF, 256), tokens[:, n].reshape(DEC, 256)], axis=0
        )
        for n in range(2)
    ]
    mine, theirs = pick(halves, core), pick(halves[::-1], core)
    received = move(theirs, dc=1)
    query_w, key_w, received = lax.optimization_barrier((query_weight, key_weight, received))
    first = gather_first(jnp.concatenate([mine, received], axis=1))
    sib_query, sib_key = move(query_w, dc=1), move(key_w, dc=1)
    value_w, *rest = lax.optimization_barrier((value_weight, *first[1:]))
    first = (first[0], *rest)
    sib_value = move(value_w, dc=1)
    second = gather_second(first)
    weights = (query_weight, key_weight, value_weight, sib_query, sib_key, sib_value)
    total = qkv(0, idx, first, weights)
    total, *second = lax.optimization_barrier((total, *second))
    third = gather_third(second)
    total = qkv(1, idx, second, weights, (total,))
    own_rows, *by_head, rows_out = qkv(2, idx, third, weights, (total,))

    heads = [move(by_head[k], dz=k) for k in (1, 3, 2)]
    one, three, two, own = lax.optimization_barrier((*heads, by_head[0]))
    blocks = (own, one, two, three)
    mine = pack(blocks)
    cross = move(mine, dxh=1, only_xh=0)
    queries = jnp.stack([a[HALF:, :256].reshape(2, DEC, 256) for a in blocks])
    other_queries = move(queries, dxh=1)
    sib = move(mine, dc=1)

    rows_out, queries, other_queries, out_w = lax.optimization_barrier(
        (rows_out, queries, other_queries, out_weight)
    )
    queries = jnp.concatenate([queries, other_queries], axis=0)
    pair = (queries[:, 0], move(queries[:, 1], dc=1))
    from_sib = move(rows_out, dc=1)
    queries = jnp.concatenate([pick(pair, core), pick(pair[::-1], core)], axis=1)
    queries = queries.reshape(256, 256)
    pair = (own_rows[HALF:], from_sib[HALF:])
    dec_rows = jnp.concatenate([pick(pair, core), pick(pair[::-1], core)], axis=0)

    spread = []
    for dy in range(4):
        at = (y + dy) % 4 * 512
        columns = jnp.concatenate(
            [
                lax.dynamic_slice_in_dim(out_w, side * 2048 + at, 512, axis=1)
                for side in (x, 1 - x)
            ],
            axis=1,
        )
        spread.append(columns if dy == 0 else move(columns, dy=dy))

    positions = (
        panel_map[:, :, None] * PANEL + jnp.arange(PANEL, dtype=jnp.int32)[None, None, :]
    )
    ok = (positions < ctx_lengths[:, None, None]).astype(F32).reshape(8, CH)
    parts = decode_parts(
        idx, stretch_lengths, queries, cache_keys, cache_values, ok, own_rows, from_sib
    )
    moved = move(parts[4:], dxh=1)
    parts, mine = lax.optimization_barrier((parts, mine))
    state = attend_own(idx, stretch_lengths, blocks, mine, sib)
    *state, moved, cross = lax.optimization_barrier((*state, moved, cross))
    cross_sib = move(cross, dc=1)
    parts = jnp.stack([parts[:4], moved])
    moved = [move(parts[:, k], dz=4 - k) for k in (1, 2, 3)]
    near, far = pack_weight(spread)
    cross_sib, near, far = lax.optimization_barrier((cross_sib, near, far))
    far = move(far, dxl=1)
    first_heads = attend_cross(
        (1, 2, 3), idx, stretch_lengths, blocks[1:], cross, cross_sib, state
    )
    first_heads, *moved = lax.optimization_barrier((first_heads, *moved))
    back_one = move(first_heads[0], dz=3)
    back_two = move(first_heads[1], dz=2)
    back_three = move(first_heads[2], dz=1)
    parts = jnp.stack([parts[:, 0], *moved], axis=1).reshape(8, 32, 384)
    dec_attn = merge_parts(parts, dec_rows)
    theirs = move(pick((dec_attn[DEC:], dec_attn[:DEC]), core), dc=1)
    dec_attn, cross = lax.optimization_barrier((dec_attn, cross))
    mine = pick((dec_attn[:DEC], dec_attn[DEC:]), core)
    last_heads = attend_cross((0,), idx, stretch_lengths, (own,), cross, cross_sib, state)
    near, last_heads = lax.optimization_barrier((near, last_heads))
    attn = head_order(idx, (last_heads[0], back_one, back_two, back_three), mine, theirs)
    first = gather_first(attn)
    attn, near = lax.optimization_barrier((attn, near))
    weights = (near, move(near, dc=1), far, move(far, dc=1))
    second = gather_second(first)
    totals = out_project(0, idx, first, weights)
    *totals, up, down, across = lax.optimization_barrier((*totals, *second))
    second = (up, down, across)
    third = gather_third(second)
    totals = out_project(1, idx, second, weights, totals)
    mine, theirs = out_project(2, idx, third, weights, totals)
    received = move(theirs, dc=1)
    pair = (mine, received)
    sides = [pick(pair, core), pick(pair[::-1], core)]
    prefill_out = jnp.stack(
        [side[:HALF].reshape(2, GROUP, 256) for side in sides], axis=1
    ).reshape(CH, 256)
    decode_out = jnp.stack(
        [side[HALF:].reshape(STEPS, 8, 256) for side in sides], axis=1
    ).reshape(STEPS, 16, 256)
    return prefill_out, decode_out


def solution(mesh):
    return jax.shard_map(
        shards,
        mesh=mesh,
        in_specs=(
            P("inst", "tp"),
            P(None, "inst", "tp"),
            P(None, "tp"),
            P(None, "tp"),
            P(None, "tp"),
            P("tp", None),
            P(None, "inst", None, "tp"),
            P(None, "inst", None, "tp"),
            P(),
            P(None, "inst"),
            P(),
        ),
        out_specs=(P("inst", "tp"), P(None, "inst", "tp")),
        check_vma=False,
    )
```

```python
import functools
import math

import jax
import jax.numpy as jnp
from jax import lax
from jax.experimental import pallas as pl
from jax.experimental.pallas import tpu as pltpu
from jax.sharding import PartitionSpec as P

HD = 128
CH = 1024
PANEL = 16
STEPS = 2
NEGATIVE = -1e30
SCALE = math.log2(math.e) / math.sqrt(HD)
AX = ("inst", "tp")
HALF = 512
GROUP = 256
DEC = 16
ROWS = HALF + DEC
CUT = 256
BF = jnp.bfloat16
F32 = jnp.float32
MIB = 1 << 20


def perm(dxh=0, dz=0, dxl=0, dy=0, dc=0, only_xh=None, zxor=0):
    pairs = []
    for xh in range(2):
        if only_xh is not None and xh != only_xh:
            continue
        for z in range(4):
            for xl in range(2):
                for y in range(4):
                    for c in range(2):
                        source = (xh * 4 + z) * 16 + xl * 8 + y * 2 + c
                        target = (
                            ((xh ^ dxh) * 4 + (((z + dz) % 4) ^ zxor)) * 16
                            + (xl ^ dxl) * 8
                            + ((y + dy) % 4) * 2
                            + (c ^ dc)
                        )
                        pairs.append((source, target))
    return pairs


def move(x, **steps):
    return lax.ppermute(x, AX, perm(**steps))


LOW = slice(0, CUT)
HIGH = ROWS - CUT


def gather_first(own):
    return own, move(own, dy=1), move(own, dy=-1), move(own, dxl=1)


def gather_second(first):
    _, before, after, beside = first
    up = move(jnp.concatenate([before[LOW], beside[CUT:]]), dy=1)
    down = move(jnp.concatenate([after[CUT:], beside[CUT:]]), dy=-1)
    across = move(jnp.concatenate([before[LOW], after[LOW]]), dxl=1)
    return up, down, across


def gather_third(second):
    _, down, across = second
    return move(across[LOW], dy=1), move(down[HIGH:], dy=-1)


STEPS_OF = (
    (
        ((0, 0), (0, -1), (0, 1), (1, 0)),
        tuple((n, 0, n, 0, ROWS) for n in range(4)),
    ),
    (
        ((0, 2), (1, -1), (1, 1)),
        (
            (0, 0, 0, 0, CUT), (0, CUT, 1, CUT, HIGH),
            (1, 0, 0, CUT, HIGH), (1, HIGH, 2, CUT, HIGH),
            (2, 0, 1, 0, CUT), (2, CUT, 2, 0, CUT),
        ),
    ),
    (((1, 2),), ((0, 0, 0, 0, CUT), (1, 0, 0, CUT, HIGH))),
)


def chip_at(idx, dx, dy):
    x = idx[2]
    x = 1 - x if dx else x
    return x * 4 + lax.rem(idx[3] + dy + 4, 4)


def qkv_kernel(step, idx, *refs):
    chips, parts = STEPS_OF[step]
    count = (4, 3, 2)[step]
    pieces, weights, refs = refs[:count], refs[count : count + 6], refs[count + 6 :]
    total, refs = (refs[0], refs[1:]) if step else (None, refs)
    xs, ws, sems = refs[-3:]
    core, z = idx[0], idx[1]
    copies = []
    for n in range(6):
        for place, (dx, dy) in enumerate(chips):
            rows = pl.ds(pl.multiple_of(chip_at(idx, dx, dy) * 512, 512), 512)
            copies.append(
                pltpu.make_async_copy(
                    weights[n].at[rows, :],
                    ws.at[n, pl.ds(place * 512, 512), :],
                    sems.at[len(copies)],
                )
            )
    for copy in copies:
        copy.start()
    for n, row, place, start, size in parts:
        for half in range(2):
            side = core if half == 0 else 1 - core
            column = pl.multiple_of(place * 512 + side * 256, 256)
            xs[start : start + size, pl.ds(column, 256)] = pieces[n][
                row : row + size, half * 256 : (half + 1) * 256
            ]

    def product(n):
        for place in range(len(chips)):
            pltpu.make_async_copy(
                weights[0].at[pl.ds(0, 512), :],
                ws.at[n, pl.ds(place * 512, 512), :],
                sems.at[n * len(chips) + place],
            ).wait()
        result = jnp.dot(xs[...], ws[n], preferred_element_type=F32)
        return result if total is None else result + total[n]

    if step < 2:

        def one(n, _):
            refs[0][n] = product(n)

        lax.fori_loop(0, 6, one, None)
        return
    for n in range(6):
        result = product(n)
        y_ref, z_refs = refs[0], refs[1:5]
        rel, kind = n // 3, n % 3
        owner = core if rel == 0 else 1 - core
        if kind == 0:
            result = result * SCALE
        result = result.astype(BF)
        for head in range(2):
            slot = lax.rem(owner * 2 + head - z + 4, 4)
            for k in range(4):

                @pl.when(slot == k)
                def _():
                    z_refs[k][:HALF, kind * 128 : (kind + 1) * 128] = result[
                        :HALF, head * 128 : (head + 1) * 128
                    ]

        if kind == 0:
            rows = slice(HALF + rel * DEC, HALF + (rel + 1) * DEC)
            for z_ref in z_refs:
                z_ref[rows, :256] = result[HALF:]
                z_ref[rows, 256:] = result[HALF:, :128]
        if rel == 1:
            refs[5][:, kind * 256 : (kind + 1) * 256] = result
        else:
            y_ref[:, kind * 256 : (kind + 1) * 256] = result


def vmem_spec():
    return pl.BlockSpec(memory_space=pltpu.VMEM)


def smem_spec():
    return pl.BlockSpec(memory_space=pltpu.SMEM)


def qkv(step, idx, pieces, weights, total=()):
    chips = len(STEPS_OF[step][0])
    shape = jax.ShapeDtypeStruct((6, ROWS, 256), F32)
    if step == 2:
        shape = (
            jax.ShapeDtypeStruct((ROWS, 768), BF),
            *[jax.ShapeDtypeStruct((HALF + 2 * DEC, 384), BF)] * 4,
            jax.ShapeDtypeStruct((ROWS, 768), BF),
        )
    return pl.pallas_call(
        functools.partial(qkv_kernel, step),
        out_shape=shape,
        in_specs=[smem_spec()]
        + [vmem_spec()] * len(pieces)
        + [pl.BlockSpec(memory_space=pltpu.HBM)] * 6
        + [vmem_spec()] * len(total),
        out_specs=(vmem_spec(),) * 6 if step == 2 else vmem_spec(),
        scratch_shapes=[
            pltpu.VMEM((ROWS, chips * 512), BF),
            pltpu.VMEM((6, chips * 512, 256), BF),
            pltpu.SemaphoreType.DMA((6 * chips,)),
        ],
        compiler_params=pltpu.CompilerParams(vmem_limit_bytes=(56, 40, 18)[step] * MIB),
        cost_estimate=pl.CostEstimate(
            flops=2 * ROWS * 512 * chips * 1536, bytes_accessed=8 * MIB, transcendentals=0
        ),
        name="qkv",
    )(idx, *pieces, *weights, *total)


def pack_kernel(a, b, c, d, out_ref):
    for n, piece in enumerate((a, b, c, d)):
        out_ref[n * HALF : (n + 1) * HALF, :] = piece[:HALF, 128:]


def pack(pieces):
    return pl.pallas_call(
        pack_kernel,
        out_shape=jax.ShapeDtypeStruct((4 * HALF, 256), BF),
        in_specs=[vmem_spec()] * 4,
        out_specs=vmem_spec(),
        compiler_params=pltpu.CompilerParams(vmem_limit_bytes=8 * MIB),
        cost_estimate=pl.CostEstimate(flops=0, bytes_accessed=4 * MIB, transcendentals=0),
        name="pack",
    )(*pieces)


def pack_weight_kernel(a, b, c, d, near_ref, far_ref):
    for n, piece in enumerate((a, b, c, d)):
        near_ref[n * 256 : (n + 1) * 256, :] = piece[:, :512]
        far_ref[n * 256 : (n + 1) * 256, :] = piece[:, 512:]


def pack_weight(pieces):
    return pl.pallas_call(
        pack_weight_kernel,
        out_shape=(jax.ShapeDtypeStruct((1024, 512), BF),) * 2,
        in_specs=[vmem_spec()] * 4,
        out_specs=(vmem_spec(),) * 2,
        compiler_params=pltpu.CompilerParams(vmem_limit_bytes=8 * MIB),
        cost_estimate=pl.CostEstimate(flops=0, bytes_accessed=4 * MIB, transcendentals=0),
        name="pack_weight",
    )(*pieces)


QT = 256
KT = 1024
PACKED = 5 * CH + 256


def wide(a, n):
    return jnp.concatenate([a] * n, axis=1)


def place_keys(idx, lens, base, mine, sib, ks, vs, offs):
    core, z = idx[0], idx[1]

    def block(b, offset):
        used = lens[base + b]
        row0 = pl.multiple_of(lax.rem(z - b + 4, 4) * HALF, HALF)
        offset = pl.multiple_of(offset, 16)
        offs[b] = offset
        first_mine = mine[pl.ds(row0, 16), :128].astype(F32)[:1]
        first_sib = sib[pl.ds(row0, 16), :128].astype(F32)[:1]
        filler = jnp.where(core == 0, first_mine, first_sib)
        for rel, source in enumerate((mine, sib)):
            side = core if rel == 0 else 1 - core
            for g in range(2):
                slot = g * 512 + side * 256
                rows = pl.ds(row0 + g * 256, 256)
                at = pl.ds(pl.multiple_of(offset + slot, 16), 256)

                @pl.when(slot + 256 <= used)
                def _():
                    ks[at, :] = source[rows, :128]
                    vs[at, :128] = source[rows, 128:]
                    vs[at, 128:] = jnp.ones((256, 128), BF)

                @pl.when((slot < used) & (slot + 256 > used))
                def _():
                    live = slot + lax.broadcasted_iota(jnp.int32, (256, 128), 0) < used
                    keys = source[rows, :128].astype(F32)
                    values = source[rows, 128:].astype(F32)
                    ks[at, :] = jnp.where(live, keys, filler).astype(BF)
                    vs[at, :128] = jnp.where(live, values, 0.0).astype(BF)
                    vs[at, 128:] = jnp.where(live, 1.0, 0.0).astype(BF)

        return offset + (used + 15) // 16 * 16

    end = lax.fori_loop(0, 4, block, 0)
    vs[pl.ds(pl.multiple_of(end, 16), KT), :] = jnp.zeros((KT, 256), BF)
    return end


def fold_tile(q, ks, vs, t, m_ref, acc_ref, i, limit_of):
    start = pl.multiple_of(t * KT, KT)
    keys = ks[pl.ds(start, KT), :]
    values = vs[pl.ds(start, KT), :]
    scores = [
        lax.dot_general(a, keys, (((1,), (1,)), ((), ())), preferred_element_type=F32) for a in q
    ]
    for g, s in enumerate(scores):
        if limit_of is not None:
            key = lax.broadcasted_iota(jnp.int32, (QT, KT), 1)
            s = jnp.where(key < limit_of(g) - start, s, NEGATIVE)
        rows = slice(g * QT, (g + 1) * QT)
        old = m_ref[i, rows]
        new = jnp.maximum(old, jnp.broadcast_to(jnp.max(s, axis=1, keepdims=True), (QT, 128)))
        p = jnp.exp2(s - wide(new, KT // 128)).astype(BF)
        acc_ref[i, rows] = acc_ref[i, rows] * wide(jnp.exp2(old - new), 2) + jnp.dot(
            p, values, preferred_element_type=F32
        )
        m_ref[i, rows] = new


def used_blocks(idx, lens, first, count, body):
    def one(i, _):
        block = lax.rem(idx[1] - first - i + 4, 4)
        used = lens[idx[4] * 4 + block]

        @pl.when(idx[0] * 256 < used)
        def _():
            body(i, block, used)

    lax.fori_loop(0, count, one, None)


def attend_own_kernel(idx, lens, q0, q1, q2, q3, mine, sib, acc_ref, m_ref, qs, ks, vs, offs):
    place_keys(idx, lens, idx[4] * 4, mine, sib, ks, vs, offs)
    for i, queries in enumerate((q0, q1, q2, q3)):
        qs[i] = queries[:HALF, :128]
    firsts = [g * 512 + idx[0] * 256 for g in range(2)]

    def body(i, block, used):
        offset = offs[block]
        q = [qs[i, g * QT : (g + 1) * QT, :] for g in range(2)]
        m_ref[i] = jnp.full((HALF, 128), NEGATIVE, F32)
        acc_ref[i] = jnp.zeros((HALF, 256), F32)

        def limit_of(g):
            return offset + firsts[g] + 1 + lax.broadcasted_iota(jnp.int32, (QT, KT), 0)

        limit = offset + jnp.minimum(firsts[1] + QT, used)
        whole = (offset + firsts[0] + 1) // KT
        tiles = (limit + KT - 1) // KT
        fold = functools.partial(fold_tile, q, ks, vs)
        lax.fori_loop(0, whole, lambda t, _: fold(t, m_ref, acc_ref, i, None), None)
        lax.fori_loop(whole, tiles, lambda t, _: fold(t, m_ref, acc_ref, i, limit_of), None)

    used_blocks(idx, lens, 0, 4, body)


def attend_own(idx, lens, pieces, mine, sib):
    return pl.pallas_call(
        attend_own_kernel,
        out_shape=(
            jax.ShapeDtypeStruct((4, HALF, 256), F32),
            jax.ShapeDtypeStruct((4, HALF, 128), F32),
        ),
        in_specs=[smem_spec()] * 2 + [vmem_spec()] * 6,
        out_specs=(vmem_spec(), vmem_spec()),
        scratch_shapes=[
            pltpu.VMEM((4, HALF, 128), BF),
            pltpu.VMEM((PACKED, 128), BF),
            pltpu.VMEM((PACKED, 256), BF),
            pltpu.SMEM((4,), jnp.int32),
        ],
        compiler_params=pltpu.CompilerParams(vmem_limit_bytes=24 * MIB),
        cost_estimate=pl.CostEstimate(
            flops=4 * CH * CH * 512, bytes_accessed=4 * MIB, transcendentals=4 * CH * CH
        ),
        name="attend_own",
    )(idx, lens, *pieces, mine, sib)


def attend_cross_kernel(which, idx, lens, *refs):
    count = len(which)
    pieces = refs[:count]
    mine, sib, acc_in, m_in, o_ref, qs, ks, vs, offs, m_ref, acc_ref = refs[count:]

    @pl.when(idx[4] == 1)
    def _():
        offs[4] = place_keys(idx, lens, 0, mine, sib, ks, vs, offs)

    o_ref[...] = jnp.zeros((count, HALF, 128), BF)
    for i, queries in enumerate(pieces):
        qs[i] = queries[:HALF, :128]

    def body(i, block, used):
        acc_ref[0] = acc_in[which[0] + i]

        @pl.when(idx[4] == 1)
        def _():
            end = offs[4]
            q = [qs[i, g * QT : (g + 1) * QT, :] for g in range(2)]
            m_ref[0] = m_in[which[0] + i]
            fold = functools.partial(fold_tile, q, ks, vs)
            whole = end // KT
            lax.fori_loop(0, whole, lambda t, _: fold(t, m_ref, acc_ref, 0, None), None)

            @pl.when(whole * KT < end)
            def _():
                fold(whole, m_ref, acc_ref, 0, lambda g: end)

        for g in range(2):
            rows = slice(g * QT, (g + 1) * QT)
            row = g * 512 + idx[0] * 256 + lax.broadcasted_iota(jnp.int32, (QT, 128), 0)
            out = acc_ref[0, rows, :128] / acc_ref[0, rows, 128:]
            o_ref[i, rows, :] = jnp.where(row < used, out, 0.0).astype(BF)

    used_blocks(idx, lens, which[0], count, body)


def attend_cross(which, idx, lens, pieces, mine, sib, state):
    return pl.pallas_call(
        functools.partial(attend_cross_kernel, which),
        out_shape=jax.ShapeDtypeStruct((len(which), HALF, 128), BF),
        in_specs=[smem_spec()] * 2 + [vmem_spec()] * (len(which) + 4),
        out_specs=vmem_spec(),
        scratch_shapes=[
            pltpu.VMEM((len(which), HALF, 128), BF),
            pltpu.VMEM((PACKED, 128), BF),
            pltpu.VMEM((PACKED, 256), BF),
            pltpu.SMEM((5,), jnp.int32),
            pltpu.VMEM((1, HALF, 128), F32),
            pltpu.VMEM((1, HALF, 256), F32),
        ],
        compiler_params=pltpu.CompilerParams(vmem_limit_bytes=24 * MIB),
        cost_estimate=pl.CostEstimate(
            flops=4 * CH * CH * 512, bytes_accessed=4 * MIB, transcendentals=4 * CH * CH
        ),
        name="attend_cross",
    )(idx, lens, *pieces, mine, sib, *state)


def decode_kernel(idx, lens, q_ref, keys, values, ok_ref, own, sib, out_ref, kc, vc, tops, sums, outs, sems):
    core, me = idx[0], idx[5]
    used = lens[me]

    def loads(n):
        home = (idx[4] ^ (n // 4)) * 4 + lax.rem(idx[1] - lax.rem(n, 4) + 4, 4)
        rows = pl.ds(pl.multiple_of(home * 16, 16), 16)
        return home, (
            pltpu.make_async_copy(keys.at[rows], kc.at[n], sems.at[2 * n]),
            pltpu.make_async_copy(values.at[rows], vc.at[n], sems.at[2 * n + 1]),
        )

    for n in range(8):
        for load in loads(n)[1]:
            load.start()
    nt = (((1,), (1,)), ((), ()))
    at = lax.broadcasted_iota(jnp.int32, (256, HALF), 1)
    slot = (at // 256) * 512 + at % 256
    ok_own = slot + core * 256 < used
    ok_sib = slot + (1 - core) * 256 < used
    for head in range(2):
        cols = slice(head * 128, (head + 1) * 128)
        kcols = slice(256 + head * 128, 256 + (head + 1) * 128)
        vcols = slice(512 + head * 128, 512 + (head + 1) * 128)
        q = q_ref[:, cols]
        s_o = lax.dot_general(q, own[:HALF, kcols], nt, preferred_element_type=F32)
        s_s = lax.dot_general(q, sib[:HALF, kcols], nt, preferred_element_type=F32)
        s_o = jnp.where(ok_own, s_o, NEGATIVE)
        s_s = jnp.where(ok_sib, s_s, NEGATIVE)
        top = jnp.maximum(
            jnp.max(s_o, axis=1, keepdims=True), jnp.max(s_s, axis=1, keepdims=True)
        )
        p_o = jnp.exp2(s_o - top)
        p_s = jnp.exp2(s_s - top)
        total = jnp.sum(p_o, axis=1, keepdims=True) + jnp.sum(p_s, axis=1, keepdims=True)
        out = jnp.dot(p_o.astype(BF), own[:HALF, vcols], preferred_element_type=F32) + jnp.dot(
            p_s.astype(BF), sib[:HALF, vcols], preferred_element_type=F32
        )
        tops[head] = jnp.broadcast_to(top, (256, 128))
        sums[head] = jnp.broadcast_to(total, (256, 128))
        outs[head] = out
    row = lax.broadcasted_iota(jnp.int32, (32, CH), 0)
    key = lax.broadcasted_iota(jnp.int32, (32, CH), 1)
    same = (row // 16) * 8 + row % 8 == key // 64
    lane = lax.broadcasted_iota(jnp.int32, (32, 128), 1)

    def group(n, _):
        home, copies = loads(n)
        for copy in copies:
            copy.wait()
        keys_c = kc[n].reshape(CH, 256)
        values_c = vc[n].reshape(CH, 256)
        ok = same & (ok_ref[pl.ds(home, 1), :] > 0)
        rows = pl.ds(pl.multiple_of(n * 32, 32), 32)
        stats = []
        for head in range(2):
            cols = slice(head * 128, (head + 1) * 128)
            top = tops[head, rows, :1]
            s = lax.dot_general(
                q_ref[rows, cols], keys_c[:, cols], nt, preferred_element_type=F32
            )
            s = jnp.where(ok, s, NEGATIVE)
            new = jnp.maximum(top, jnp.max(s, axis=1, keepdims=True))
            p = jnp.exp2(s - new)
            factor = jnp.exp2(top - new)
            stats += [new, factor * sums[head, rows, :1] + jnp.sum(p, axis=1, keepdims=True)]
            out_ref[n, :, cols] = factor * outs[head, rows, :] + jnp.dot(
                p.astype(BF), values_c[:, cols], preferred_element_type=F32
            )
        out_ref[n, :, 256:] = jnp.where(
            lane < 32,
            stats[0],
            jnp.where(lane < 64, stats[1], jnp.where(lane < 96, stats[2], stats[3])),
        )

    lax.fori_loop(0, 8, group, None)


def decode_parts(idx, lens, queries, cache_keys, cache_values, ok, own, sib):
    hbm = pl.BlockSpec(memory_space=pltpu.HBM)
    return pl.pallas_call(
        decode_kernel,
        out_shape=jax.ShapeDtypeStruct((8, 32, 384), F32),
        in_specs=[smem_spec()] * 2 + [vmem_spec(), hbm, hbm] + [vmem_spec()] * 3,
        out_specs=vmem_spec(),
        scratch_shapes=[
            pltpu.VMEM((8, 16, 4, PANEL, 256), BF),
            pltpu.VMEM((8, 16, 4, PANEL, 256), BF),
            *[pltpu.VMEM((2, 256, 128), F32)] * 3,
            pltpu.SemaphoreType.DMA((16,)),
        ],
        compiler_params=pltpu.CompilerParams(vmem_limit_bytes=50 * MIB),
        cost_estimate=pl.CostEstimate(
            flops=8 * 32 * 2048 * 1024, bytes_accessed=10 * MIB, transcendentals=8 * 64 * 2048
        ),
        name="decode_parts",
    )(idx, lens, queries, cache_keys, cache_values, ok, own, sib)


def merge_kernel(parts, qkv_rows, out_ref):
    for head in range(2):
        cols = slice(head * 128, (head + 1) * 128)
        tops = [parts[n, :, 256 + head * 64 : 256 + head * 64 + 1] for n in range(8)]
        sums = [parts[n, :, 288 + head * 64 : 288 + head * 64 + 1] for n in range(8)]
        for side in range(2):
            for s in range(2):
                rows = slice(side * 16 + s * 8, side * 16 + s * 8 + 8)
                q = qkv_rows[rows, cols].astype(F32)
                fresh = []
                for u in range(s + 1):
                    from_rows = slice(side * 16 + u * 8, side * 16 + u * 8 + 8)
                    k = qkv_rows[from_rows, 256 + head * 128 : 384 + head * 128].astype(F32)
                    v = qkv_rows[from_rows, 512 + head * 128 : 640 + head * 128].astype(F32)
                    fresh.append((jnp.sum(q * k, axis=1, keepdims=True), v))
                top = fresh[0][0]
                for score, _ in fresh[1:]:
                    top = jnp.maximum(top, score)
                for part in tops:
                    top = jnp.maximum(top, part[rows])
                total = jnp.zeros((8, 1), F32)
                out = jnp.zeros((8, 128), F32)
                for score, v in fresh:
                    w = jnp.exp2(score - top)
                    total += w
                    out += w.astype(BF).astype(F32) * v
                for n in range(8):
                    w = jnp.exp2(tops[n][rows] - top)
                    total += w * sums[n][rows]
                    out += w * parts[n, rows, cols]
                out_ref[rows, cols] = (out / total).astype(BF)


def merge_parts(parts, qkv_rows):
    return pl.pallas_call(
        merge_kernel,
        out_shape=jax.ShapeDtypeStruct((32, 256), BF),
        in_specs=[vmem_spec()] * 2,
        out_specs=vmem_spec(),
        compiler_params=pltpu.CompilerParams(vmem_limit_bytes=4 * MIB),
        cost_estimate=pl.CostEstimate(flops=MIB, bytes_accessed=MIB, transcendentals=1000),
        name="merge_parts",
    )(parts, qkv_rows)


def head_order_kernel(idx, a, b, c, d, near, far, out_ref):
    for k, piece in enumerate((a, b, c, d)):
        column = pl.multiple_of(lax.rem(idx[1] + k - 2 * idx[0] + 4, 4) * 128, 128)
        out_ref[:HALF, pl.ds(column, 128)] = piece[...]
    out_ref[HALF:, :256] = near[...]
    out_ref[HALF:, 256:] = far[...]


def head_order(idx, pieces, near, far):
    return pl.pallas_call(
        head_order_kernel,
        out_shape=jax.ShapeDtypeStruct((ROWS, 512), BF),
        in_specs=[smem_spec()] + [vmem_spec()] * 6,
        out_specs=vmem_spec(),
        compiler_params=pltpu.CompilerParams(vmem_limit_bytes=4 * MIB),
        cost_estimate=pl.CostEstimate(flops=0, bytes_accessed=MIB, transcendentals=0),
        name="head_order",
    )(idx, *pieces, near, far)


def out_kernel(step, idx, *refs):
    chips, parts = STEPS_OF[step]
    count = (4, 3, 2)[step]
    pieces, ws, refs = refs[:count], refs[count : count + 4], refs[count + 4 :]
    totals, refs = (refs[:2], refs[2:]) if step else (None, refs)
    results, xs = refs[:2], refs[2]
    for n, row, place, start, size in parts:
        xs[start : start + size, place * 512 : (place + 1) * 512] = pieces[n][row : row + size, :]
    for rel in range(2):
        side = idx[0] if rel == 0 else 1 - idx[0]
        columns = pl.ds(pl.multiple_of(side * 256, 256), 256)
        result = None if totals is None else totals[rel][...]
        for place, (dx, dy) in enumerate(chips):
            k = -dy % 4
            for half, w in enumerate(ws[2 * dx : 2 * dx + 2]):
                at = place * 512 + half * 256
                term = jnp.dot(
                    xs[:, at : at + 256],
                    w[k * 256 : (k + 1) * 256, columns],
                    preferred_element_type=F32,
                )
                result = term if result is None else result + term
        results[rel][...] = result


def out_project(step, idx, pieces, weights, totals=()):
    chips = len(STEPS_OF[step][0])
    return pl.pallas_call(
        functools.partial(out_kernel, step),
        out_shape=(
            jax.ShapeDtypeStruct((ROWS, 256), F32),
            jax.ShapeDtypeStruct((ROWS, 256), F32),
        ),
        in_specs=[smem_spec()] + [vmem_spec()] * (len(pieces) + 4 + len(totals)),
        out_specs=(vmem_spec(), vmem_spec()),
        scratch_shapes=[pltpu.VMEM((ROWS, chips * 512), BF)],
        compiler_params=pltpu.CompilerParams(vmem_limit_bytes=20 * MIB),
        cost_estimate=pl.CostEstimate(
            flops=2 * ROWS * 512 * chips * 512, bytes_accessed=4 * MIB, transcendentals=0
        ),
        name="out_project",
    )(idx, *pieces, *weights, *totals)


def pick(pair, core):
    return jnp.where(core == 0, pair[0], pair[1])


def shards(
    prompt,
    decode_tokens,
    query_weight,
    key_weight,
    value_weight,
    out_weight,
    cache_keys,
    cache_values,
    stretch_lengths,
    panel_map,
    ctx_lengths,
):
    inst = lax.axis_index("inst")
    tp = lax.axis_index("tp")
    core = tp % 2
    y = (tp // 2) % 4
    x = tp // 8
    z = inst % 4
    xh = inst // 4
    idx = jnp.stack([core, z, x, y, xh, inst, 0, 0]).astype(jnp.int32)

    groups = prompt.reshape(2, 2, GROUP, 256)
    tokens = decode_tokens.reshape(STEPS, 2, 8, 256)
    halves = [
        jnp.concatenate(
            [groups[:, n].reshape(HALF, 256), tokens[:, n].reshape(DEC, 256)], axis=0
        )
        for n in range(2)
    ]
    mine, theirs = pick(halves, core), pick(halves[::-1], core)
    received = move(theirs, dc=1)
    query_w, key_w, received = lax.optimization_barrier((query_weight, key_weight, received))
    first = gather_first(jnp.concatenate([mine, received], axis=1))
    sib_query, sib_key = move(query_w, dc=1), move(key_w, dc=1)
    value_w, *rest = lax.optimization_barrier((value_weight, *first[1:]))
    first = (first[0], *rest)
    sib_value = move(value_w, dc=1)
    second = gather_second(first)
    weights = (query_weight, key_weight, value_weight, sib_query, sib_key, sib_value)
    total = qkv(0, idx, first, weights)
    total, *second = lax.optimization_barrier((total, *second))
    third = gather_third(second)
    total = qkv(1, idx, second, weights, (total,))
    own_rows, *by_head, rows_out = qkv(2, idx, third, weights, (total,))

    heads = [move(by_head[k], dz=k) for k in (1, 3, 2)]
    one, three, two, own = lax.optimization_barrier((*heads, by_head[0]))
    blocks = (own, one, two, three)
    mine = pack(blocks)
    cross = move(mine, dxh=1, only_xh=0)
    queries = jnp.stack([a[HALF:, :256].reshape(2, DEC, 256) for a in blocks])
    other_queries = move(queries, dxh=1)
    sib = move(mine, dc=1)

    rows_out, queries, other_queries, out_w = lax.optimization_barrier(
        (rows_out, queries, other_queries, out_weight)
    )
    queries = jnp.concatenate([queries, other_queries], axis=0)
    pair = (queries[:, 0], move(queries[:, 1], dc=1))
    from_sib = move(rows_out, dc=1)
    queries = jnp.concatenate([pick(pair, core), pick(pair[::-1], core)], axis=1)
    queries = queries.reshape(256, 256)
    pair = (own_rows[HALF:], from_sib[HALF:])
    dec_rows = jnp.concatenate([pick(pair, core), pick(pair[::-1], core)], axis=0)

    spread = []
    for dy in range(4):
        at = (y + dy) % 4 * 512
        columns = jnp.concatenate(
            [
                lax.dynamic_slice_in_dim(out_w, side * 2048 + at, 512, axis=1)
                for side in (x, 1 - x)
            ],
            axis=1,
        )
        spread.append(columns if dy == 0 else move(columns, dy=dy))

    positions = (
        panel_map[:, :, None] * PANEL + jnp.arange(PANEL, dtype=jnp.int32)[None, None, :]
    )
    ok = (positions < ctx_lengths[:, None, None]).astype(F32).reshape(8, CH)
    parts = decode_parts(
        idx, stretch_lengths, queries, cache_keys, cache_values, ok, own_rows, from_sib
    )
    moved = move(parts[4:], dxh=1)
    parts, mine = lax.optimization_barrier((parts, mine))
    state = attend_own(idx, stretch_lengths, blocks, mine, sib)
    acc, top, *spread = lax.optimization_barrier((*state, *spread))
    acc, top, moved, cross, near, far = lax.optimization_barrier(
        (acc, top, moved, cross, *pack_weight(spread))
    )
    state = (acc, top)
    cross_sib = move(cross, dc=1)
    parts = jnp.stack([parts[:4], moved])
    moved = [move(parts[:, k], dz=4 - k) for k in (1, 2, 3)]
    far = move(far, dxl=1)
    first_heads = attend_cross(
        (1, 2, 3), idx, stretch_lengths, blocks[1:], cross, cross_sib, state
    )
    first_heads, *moved = lax.optimization_barrier((first_heads, *moved))
    back_one = move(first_heads[0], dz=3)
    back_two = move(first_heads[1], dz=2)
    back_three = move(first_heads[2], dz=1)
    parts = jnp.stack([parts[:, 0], *moved], axis=1).reshape(8, 32, 384)
    dec_attn = merge_parts(parts, dec_rows)
    theirs = move(pick((dec_attn[DEC:], dec_attn[:DEC]), core), dc=1)
    dec_attn, cross = lax.optimization_barrier((dec_attn, cross))
    mine = pick((dec_attn[:DEC], dec_attn[DEC:]), core)
    last_heads = attend_cross((0,), idx, stretch_lengths, (own,), cross, cross_sib, state)
    near, last_heads = lax.optimization_barrier((near, last_heads))
    attn = head_order(idx, (last_heads[0], back_one, back_two, back_three), mine, theirs)
    first = gather_first(attn)
    attn, near = lax.optimization_barrier((attn, near))
    weights = (near, move(near, dc=1), far, move(far, dc=1))
    second = gather_second(first)
    totals = out_project(0, idx, first, weights)
    *totals, up, down, across = lax.optimization_barrier((*totals, *second))
    second = (up, down, across)
    third = gather_third(second)
    totals = out_project(1, idx, second, weights, totals)
    mine, theirs = out_project(2, idx, third, weights, totals)
    received = move(theirs, dc=1)
    pair = (mine, received)
    sides = [pick(pair, core), pick(pair[::-1], core)]
    prefill_out = jnp.stack(
        [side[:HALF].reshape(2, GROUP, 256) for side in sides], axis=1
    ).reshape(CH, 256)
    decode_out = jnp.stack(
        [side[HALF:].reshape(STEPS, 8, 256) for side in sides], axis=1
    ).reshape(STEPS, 16, 256)
    return prefill_out, decode_out


def solution(mesh):
    return jax.shard_map(
        shards,
        mesh=mesh,
        in_specs=(
            P("inst", "tp"),
            P(None, "inst", "tp"),
            P(None, "tp"),
            P(None, "tp"),
            P(None, "tp"),
            P("tp", None),
            P(None, "inst", None, "tp"),
            P(None, "inst", None, "tp"),
            P(),
            P(None, "inst"),
            P(),
        ),
        out_specs=(P("inst", "tp"), P(None, "inst", "tp")),
        check_vma=False,
    )
```

```python
import functools
import math

import jax
import jax.numpy as jnp
from jax import lax
from jax.experimental import pallas as pl
from jax.experimental.pallas import tpu as pltpu
from jax.sharding import PartitionSpec as P

HD = 128
CH = 1024
PANEL = 16
STEPS = 2
NEGATIVE = -1e30
SCALE = math.log2(math.e) / math.sqrt(HD)
AX = ("inst", "tp")
HALF = 512
GROUP = 256
DEC = 16
ROWS = HALF + DEC
CUT = 256
BF = jnp.bfloat16
F32 = jnp.float32
MIB = 1 << 20


def perm(dxh=0, dz=0, dxl=0, dy=0, dc=0, only_xh=None, zxor=0):
    pairs = []
    for xh in range(2):
        if only_xh is not None and xh != only_xh:
            continue
        for z in range(4):
            for xl in range(2):
                for y in range(4):
                    for c in range(2):
                        source = (xh * 4 + z) * 16 + xl * 8 + y * 2 + c
                        target = (
                            ((xh ^ dxh) * 4 + (((z + dz) % 4) ^ zxor)) * 16
                            + (xl ^ dxl) * 8
                            + ((y + dy) % 4) * 2
                            + (c ^ dc)
                        )
                        pairs.append((source, target))
    return pairs


def move(x, **steps):
    return lax.ppermute(x, AX, perm(**steps))


LOW = slice(0, CUT)
HIGH = ROWS - CUT


def gather_first(own):
    return own, move(own, dy=1), move(own, dy=-1), move(own, dxl=1)


def gather_second(first):
    _, before, after, beside = first
    up = move(jnp.concatenate([before[LOW], beside[CUT:]]), dy=1)
    down = move(jnp.concatenate([after[CUT:], beside[CUT:]]), dy=-1)
    across = move(jnp.concatenate([before[LOW], after[LOW]]), dxl=1)
    return up, down, across


def gather_third(second):
    _, down, across = second
    return move(across[LOW], dy=1), move(down[HIGH:], dy=-1)


STEPS_OF = (
    (
        ((0, 0), (0, -1), (0, 1), (1, 0)),
        tuple((n, 0, n, 0, ROWS) for n in range(4)),
    ),
    (
        ((0, 2), (1, -1), (1, 1)),
        (
            (0, 0, 0, 0, CUT), (0, CUT, 1, CUT, HIGH),
            (1, 0, 0, CUT, HIGH), (1, HIGH, 2, CUT, HIGH),
            (2, 0, 1, 0, CUT), (2, CUT, 2, 0, CUT),
        ),
    ),
    (((1, 2),), ((0, 0, 0, 0, CUT), (1, 0, 0, CUT, HIGH))),
)


def chip_at(idx, dx, dy):
    x = idx[2]
    x = 1 - x if dx else x
    return x * 4 + lax.rem(idx[3] + dy + 4, 4)


def qkv_kernel(step, idx, *refs):
    chips, parts = STEPS_OF[step]
    count = (4, 3, 2)[step]
    pieces, weights, refs = refs[:count], refs[count : count + 6], refs[count + 6 :]
    total, refs = (refs[0], refs[1:]) if step else (None, refs)
    xs, ws, sems = refs[-3:]
    core, z = idx[0], idx[1]
    copies = []
    for n in range(6):
        for place, (dx, dy) in enumerate(chips):
            rows = pl.ds(pl.multiple_of(chip_at(idx, dx, dy) * 512, 512), 512)
            copies.append(
                pltpu.make_async_copy(
                    weights[n].at[rows, :],
                    ws.at[n, pl.ds(place * 512, 512), :],
                    sems.at[len(copies)],
                )
            )
    for copy in copies:
        copy.start()
    for n, row, place, start, size in parts:
        for half in range(2):
            side = core if half == 0 else 1 - core
            column = pl.multiple_of(place * 512 + side * 256, 256)
            xs[start : start + size, pl.ds(column, 256)] = pieces[n][
                row : row + size, half * 256 : (half + 1) * 256
            ]

    def product(n):
        for place in range(len(chips)):
            pltpu.make_async_copy(
                weights[0].at[pl.ds(0, 512), :],
                ws.at[n, pl.ds(place * 512, 512), :],
                sems.at[n * len(chips) + place],
            ).wait()
        result = jnp.dot(xs[...], ws[n], preferred_element_type=F32)
        return result if total is None else result + total[n]

    if step < 2:

        def one(n, _):
            refs[0][n] = product(n)

        lax.fori_loop(0, 6, one, None)
        return
    y_ref, z_refs, sib_ref = refs[0], refs[1:5], refs[5]

    def side(rel, _):
        owner = jnp.where(rel == 0, core, 1 - core)
        rows = pl.ds(pl.multiple_of(HALF + rel * DEC, DEC), DEC)
        for kind in range(3):
            result = product(rel * 3 + kind)
            if kind == 0:
                result = result * SCALE
            result = result.astype(BF)
            for k in range(4):
                for head in range(2):

                    @pl.when(lax.rem(owner * 2 + head - z + 4, 4) == k)
                    def _():
                        z_refs[k][:HALF, kind * 128 : (kind + 1) * 128] = result[
                            :HALF, head * 128 : (head + 1) * 128
                        ]

                if kind == 0:
                    z_refs[k][rows, :256] = result[HALF:]
                    z_refs[k][rows, 256:] = result[HALF:, :128]
            for index, target in enumerate((y_ref, sib_ref)):

                @pl.when(rel == index)
                def _():
                    target[:, kind * 256 : (kind + 1) * 256] = result

    lax.fori_loop(0, 2, side, None)


def vmem_spec():
    return pl.BlockSpec(memory_space=pltpu.VMEM)


def smem_spec():
    return pl.BlockSpec(memory_space=pltpu.SMEM)


def qkv(step, idx, pieces, weights, total=()):
    chips = len(STEPS_OF[step][0])
    shape = jax.ShapeDtypeStruct((6, ROWS, 256), F32)
    if step == 2:
        shape = (
            jax.ShapeDtypeStruct((ROWS, 768), BF),
            *[jax.ShapeDtypeStruct((HALF + 2 * DEC, 384), BF)] * 4,
            jax.ShapeDtypeStruct((ROWS, 768), BF),
        )
    return pl.pallas_call(
        functools.partial(qkv_kernel, step),
        out_shape=shape,
        in_specs=[smem_spec()]
        + [vmem_spec()] * len(pieces)
        + [pl.BlockSpec(memory_space=pltpu.HBM)] * 6
        + [vmem_spec()] * len(total),
        out_specs=(vmem_spec(),) * 6 if step == 2 else vmem_spec(),
        scratch_shapes=[
            pltpu.VMEM((ROWS, chips * 512), BF),
            pltpu.VMEM((6, chips * 512, 256), BF),
            pltpu.SemaphoreType.DMA((6 * chips,)),
        ],
        compiler_params=pltpu.CompilerParams(vmem_limit_bytes=(56, 40, 18)[step] * MIB),
        cost_estimate=pl.CostEstimate(
            flops=2 * ROWS * 512 * chips * 1536, bytes_accessed=8 * MIB, transcendentals=0
        ),
        name="qkv",
    )(idx, *pieces, *weights, *total)


def pack_kernel(a, b, c, d, out_ref):
    for n, piece in enumerate((a, b, c, d)):
        out_ref[n * HALF : (n + 1) * HALF, :] = piece[:HALF, 128:]


def pack(pieces):
    return pl.pallas_call(
        pack_kernel,
        out_shape=jax.ShapeDtypeStruct((4 * HALF, 256), BF),
        in_specs=[vmem_spec()] * 4,
        out_specs=vmem_spec(),
        compiler_params=pltpu.CompilerParams(vmem_limit_bytes=8 * MIB),
        cost_estimate=pl.CostEstimate(flops=0, bytes_accessed=4 * MIB, transcendentals=0),
        name="pack",
    )(*pieces)


def pack_weight_kernel(a, b, c, d, near_ref, far_ref):
    for n, piece in enumerate((a, b, c, d)):
        near_ref[n * 256 : (n + 1) * 256, :] = piece[:, :512]
        far_ref[n * 256 : (n + 1) * 256, :] = piece[:, 512:]


def pack_weight(pieces):
    return pl.pallas_call(
        pack_weight_kernel,
        out_shape=(jax.ShapeDtypeStruct((1024, 512), BF),) * 2,
        in_specs=[vmem_spec()] * 4,
        out_specs=(vmem_spec(),) * 2,
        compiler_params=pltpu.CompilerParams(vmem_limit_bytes=8 * MIB),
        cost_estimate=pl.CostEstimate(flops=0, bytes_accessed=4 * MIB, transcendentals=0),
        name="pack_weight",
    )(*pieces)


QT = 256
KT = 1024
PACKED = 5 * CH + 256


def wide(a, n):
    return jnp.concatenate([a] * n, axis=1)


def place_keys(idx, lens, base, mine, sib, ks, vs, offs):
    core, z = idx[0], idx[1]

    def block(b, offset):
        used = lens[base + b]
        row0 = pl.multiple_of(lax.rem(z - b + 4, 4) * HALF, HALF)
        offset = pl.multiple_of(offset, 16)
        offs[b] = offset
        first_mine = mine[pl.ds(row0, 16), :128].astype(F32)[:1]
        first_sib = sib[pl.ds(row0, 16), :128].astype(F32)[:1]
        filler = jnp.where(core == 0, first_mine, first_sib)
        for rel, source in enumerate((mine, sib)):
            side = core if rel == 0 else 1 - core
            for g in range(2):
                slot = g * 512 + side * 256
                rows = pl.ds(row0 + g * 256, 256)
                at = pl.ds(pl.multiple_of(offset + slot, 16), 256)

                @pl.when(slot + 256 <= used)
                def _():
                    ks[at, :] = source[rows, :128]
                    vs[at, :128] = source[rows, 128:]
                    vs[at, 128:] = jnp.ones((256, 128), BF)

                @pl.when((slot < used) & (slot + 256 > used))
                def _():
                    live = slot + lax.broadcasted_iota(jnp.int32, (256, 128), 0) < used
                    keys = source[rows, :128].astype(F32)
                    values = source[rows, 128:].astype(F32)
                    ks[at, :] = jnp.where(live, keys, filler).astype(BF)
                    vs[at, :128] = jnp.where(live, values, 0.0).astype(BF)
                    vs[at, 128:] = jnp.where(live, 1.0, 0.0).astype(BF)

        return offset + (used + 15) // 16 * 16

    end = lax.fori_loop(0, 4, block, 0)
    vs[pl.ds(pl.multiple_of(end, 16), KT), :] = jnp.zeros((KT, 256), BF)
    return end


def fold_tile(q, ks, vs, t, m_ref, acc_ref, i, limit_of):
    start = pl.multiple_of(t * KT, KT)
    keys = ks[pl.ds(start, KT), :]
    values = vs[pl.ds(start, KT), :]
    scores = [
        lax.dot_general(a, keys, (((1,), (1,)), ((), ())), preferred_element_type=F32) for a in q
    ]
    for g, s in enumerate(scores):
        if limit_of is not None:
            key = lax.broadcasted_iota(jnp.int32, (QT, KT), 1)
            s = jnp.where(key < limit_of(g) - start, s, NEGATIVE)
        rows = slice(g * QT, (g + 1) * QT)
        old = m_ref[i, rows]
        new = jnp.maximum(old, jnp.broadcast_to(jnp.max(s, axis=1, keepdims=True), (QT, 128)))
        p = jnp.exp2(s - wide(new, KT // 128)).astype(BF)
        acc_ref[i, rows] = acc_ref[i, rows] * wide(jnp.exp2(old - new), 2) + jnp.dot(
            p, values, preferred_element_type=F32
        )
        m_ref[i, rows] = new


def used_blocks(idx, lens, first, count, body):
    def one(i, _):
        block = lax.rem(idx[1] - first - i + 4, 4)
        used = lens[idx[4] * 4 + block]

        @pl.when(idx[0] * 256 < used)
        def _():
            body(i, block, used)

    lax.fori_loop(0, count, one, None)


def attend_own_kernel(idx, lens, q0, q1, q2, q3, mine, sib, acc_ref, m_ref, qs, ks, vs, offs):
    place_keys(idx, lens, idx[4] * 4, mine, sib, ks, vs, offs)
    for i, queries in enumerate((q0, q1, q2, q3)):
        qs[i] = queries[:HALF, :128]
    firsts = [g * 512 + idx[0] * 256 for g in range(2)]

    def body(i, block, used):
        offset = offs[block]
        q = [qs[i, g * QT : (g + 1) * QT, :] for g in range(2)]
        m_ref[i] = jnp.full((HALF, 128), NEGATIVE, F32)
        acc_ref[i] = jnp.zeros((HALF, 256), F32)

        def limit_of(g):
            return offset + firsts[g] + 1 + lax.broadcasted_iota(jnp.int32, (QT, KT), 0)

        limit = offset + jnp.minimum(firsts[1] + QT, used)
        whole = (offset + firsts[0] + 1) // KT
        tiles = (limit + KT - 1) // KT
        fold = functools.partial(fold_tile, q, ks, vs)
        lax.fori_loop(0, whole, lambda t, _: fold(t, m_ref, acc_ref, i, None), None)
        lax.fori_loop(whole, tiles, lambda t, _: fold(t, m_ref, acc_ref, i, limit_of), None)

    used_blocks(idx, lens, 0, 4, body)


def attend_own(idx, lens, pieces, mine, sib):
    return pl.pallas_call(
        attend_own_kernel,
        out_shape=(
            jax.ShapeDtypeStruct((4, HALF, 256), F32),
            jax.ShapeDtypeStruct((4, HALF, 128), F32),
        ),
        in_specs=[smem_spec()] * 2 + [vmem_spec()] * 6,
        out_specs=(vmem_spec(), vmem_spec()),
        scratch_shapes=[
            pltpu.VMEM((4, HALF, 128), BF),
            pltpu.VMEM((PACKED, 128), BF),
            pltpu.VMEM((PACKED, 256), BF),
            pltpu.SMEM((4,), jnp.int32),
        ],
        compiler_params=pltpu.CompilerParams(vmem_limit_bytes=24 * MIB),
        cost_estimate=pl.CostEstimate(
            flops=4 * CH * CH * 512, bytes_accessed=4 * MIB, transcendentals=4 * CH * CH
        ),
        name="attend_own",
    )(idx, lens, *pieces, mine, sib)


def attend_cross_kernel(which, idx, lens, *refs):
    count = len(which)
    pieces = refs[:count]
    mine, sib, acc_in, m_in, o_ref, qs, ks, vs, offs, m_ref, acc_ref = refs[count:]

    @pl.when(idx[4] == 1)
    def _():
        offs[4] = place_keys(idx, lens, 0, mine, sib, ks, vs, offs)

    o_ref[...] = jnp.zeros((count, HALF, 128), BF)
    for i, queries in enumerate(pieces):
        qs[i] = queries[:HALF, :128]

    def body(i, block, used):
        acc_ref[0] = acc_in[which[0] + i]

        @pl.when(idx[4] == 1)
        def _():
            end = offs[4]
            q = [qs[i, g * QT : (g + 1) * QT, :] for g in range(2)]
            m_ref[0] = m_in[which[0] + i]
            fold = functools.partial(fold_tile, q, ks, vs)
            whole = end // KT
            lax.fori_loop(0, whole, lambda t, _: fold(t, m_ref, acc_ref, 0, None), None)

            @pl.when(whole * KT < end)
            def _():
                fold(whole, m_ref, acc_ref, 0, lambda g: end)

        for g in range(2):
            rows = slice(g * QT, (g + 1) * QT)
            row = g * 512 + idx[0] * 256 + lax.broadcasted_iota(jnp.int32, (QT, 128), 0)
            out = acc_ref[0, rows, :128] / acc_ref[0, rows, 128:]
            o_ref[i, rows, :] = jnp.where(row < used, out, 0.0).astype(BF)

    used_blocks(idx, lens, which[0], count, body)


def attend_cross(which, idx, lens, pieces, mine, sib, state):
    return pl.pallas_call(
        functools.partial(attend_cross_kernel, which),
        out_shape=jax.ShapeDtypeStruct((len(which), HALF, 128), BF),
        in_specs=[smem_spec()] * 2 + [vmem_spec()] * (len(which) + 4),
        out_specs=vmem_spec(),
        scratch_shapes=[
            pltpu.VMEM((len(which), HALF, 128), BF),
            pltpu.VMEM((PACKED, 128), BF),
            pltpu.VMEM((PACKED, 256), BF),
            pltpu.SMEM((5,), jnp.int32),
            pltpu.VMEM((1, HALF, 128), F32),
            pltpu.VMEM((1, HALF, 256), F32),
        ],
        compiler_params=pltpu.CompilerParams(vmem_limit_bytes=24 * MIB),
        cost_estimate=pl.CostEstimate(
            flops=4 * CH * CH * 512, bytes_accessed=4 * MIB, transcendentals=4 * CH * CH
        ),
        name="attend_cross",
    )(idx, lens, *pieces, mine, sib, *state)


def decode_kernel(idx, lens, q_ref, keys, values, ok_ref, own, sib, out_ref, kc, vc, tops, sums, outs, sems):
    core, me = idx[0], idx[5]
    used = lens[me]

    def loads(n):
        home = (idx[4] ^ (n // 4)) * 4 + lax.rem(idx[1] - lax.rem(n, 4) + 4, 4)
        rows = pl.ds(pl.multiple_of(home * 16, 16), 16)
        return home, (
            pltpu.make_async_copy(keys.at[rows], kc.at[n], sems.at[2 * n]),
            pltpu.make_async_copy(values.at[rows], vc.at[n], sems.at[2 * n + 1]),
        )

    for n in range(8):
        for load in loads(n)[1]:
            load.start()
    nt = (((1,), (1,)), ((), ()))
    at = lax.broadcasted_iota(jnp.int32, (256, HALF), 1)
    slot = (at // 256) * 512 + at % 256
    ok_own = slot + core * 256 < used
    ok_sib = slot + (1 - core) * 256 < used
    for head in range(2):
        cols = slice(head * 128, (head + 1) * 128)
        kcols = slice(256 + head * 128, 256 + (head + 1) * 128)
        vcols = slice(512 + head * 128, 512 + (head + 1) * 128)
        q = q_ref[:, cols]
        s_o = lax.dot_general(q, own[:HALF, kcols], nt, preferred_element_type=F32)
        s_s = lax.dot_general(q, sib[:HALF, kcols], nt, preferred_element_type=F32)
        s_o = jnp.where(ok_own, s_o, NEGATIVE)
        s_s = jnp.where(ok_sib, s_s, NEGATIVE)
        top = jnp.maximum(
            jnp.max(s_o, axis=1, keepdims=True), jnp.max(s_s, axis=1, keepdims=True)
        )
        p_o = jnp.exp2(s_o - top)
        p_s = jnp.exp2(s_s - top)
        total = jnp.sum(p_o, axis=1, keepdims=True) + jnp.sum(p_s, axis=1, keepdims=True)
        out = jnp.dot(p_o.astype(BF), own[:HALF, vcols], preferred_element_type=F32) + jnp.dot(
            p_s.astype(BF), sib[:HALF, vcols], preferred_element_type=F32
        )
        tops[head] = jnp.broadcast_to(top, (256, 128))
        sums[head] = jnp.broadcast_to(total, (256, 128))
        outs[head] = out
    row = lax.broadcasted_iota(jnp.int32, (32, CH), 0)
    key = lax.broadcasted_iota(jnp.int32, (32, CH), 1)
    same = (row // 16) * 8 + row % 8 == key // 64
    lane = lax.broadcasted_iota(jnp.int32, (32, 128), 1)

    def group(n, _):
        home, copies = loads(n)
        for copy in copies:
            copy.wait()
        keys_c = kc[n].reshape(CH, 256)
        values_c = vc[n].reshape(CH, 256)
        ok = same & (ok_ref[pl.ds(home, 1), :] > 0)
        rows = pl.ds(pl.multiple_of(n * 32, 32), 32)
        stats = []
        for head in range(2):
            cols = slice(head * 128, (head + 1) * 128)
            top = tops[head, rows, :1]
            s = lax.dot_general(
                q_ref[rows, cols], keys_c[:, cols], nt, preferred_element_type=F32
            )
            s = jnp.where(ok, s, NEGATIVE)
            new = jnp.maximum(top, jnp.max(s, axis=1, keepdims=True))
            p = jnp.exp2(s - new)
            factor = jnp.exp2(top - new)
            stats += [new, factor * sums[head, rows, :1] + jnp.sum(p, axis=1, keepdims=True)]
            out_ref[n, :, cols] = factor * outs[head, rows, :] + jnp.dot(
                p.astype(BF), values_c[:, cols], preferred_element_type=F32
            )
        out_ref[n, :, 256:] = jnp.where(
            lane < 32,
            stats[0],
            jnp.where(lane < 64, stats[1], jnp.where(lane < 96, stats[2], stats[3])),
        )

    lax.fori_loop(0, 8, group, None)


def decode_parts(idx, lens, queries, cache_keys, cache_values, ok, own, sib):
    hbm = pl.BlockSpec(memory_space=pltpu.HBM)
    return pl.pallas_call(
        decode_kernel,
        out_shape=jax.ShapeDtypeStruct((8, 32, 384), F32),
        in_specs=[smem_spec()] * 2 + [vmem_spec(), hbm, hbm] + [vmem_spec()] * 3,
        out_specs=vmem_spec(),
        scratch_shapes=[
            pltpu.VMEM((8, 16, 4, PANEL, 256), BF),
            pltpu.VMEM((8, 16, 4, PANEL, 256), BF),
            *[pltpu.VMEM((2, 256, 128), F32)] * 3,
            pltpu.SemaphoreType.DMA((16,)),
        ],
        compiler_params=pltpu.CompilerParams(vmem_limit_bytes=50 * MIB),
        cost_estimate=pl.CostEstimate(
            flops=8 * 32 * 2048 * 1024, bytes_accessed=10 * MIB, transcendentals=8 * 64 * 2048
        ),
        name="decode_parts",
    )(idx, lens, queries, cache_keys, cache_values, ok, own, sib)


def merge_kernel(parts, qkv_rows, out_ref):
    for head in range(2):
        cols = slice(head * 128, (head + 1) * 128)
        tops = [parts[n, :, 256 + head * 64 : 256 + head * 64 + 1] for n in range(8)]
        sums = [parts[n, :, 288 + head * 64 : 288 + head * 64 + 1] for n in range(8)]
        for side in range(2):
            for s in range(2):
                rows = slice(side * 16 + s * 8, side * 16 + s * 8 + 8)
                q = qkv_rows[rows, cols].astype(F32)
                fresh = []
                for u in range(s + 1):
                    from_rows = slice(side * 16 + u * 8, side * 16 + u * 8 + 8)
                    k = qkv_rows[from_rows, 256 + head * 128 : 384 + head * 128].astype(F32)
                    v = qkv_rows[from_rows, 512 + head * 128 : 640 + head * 128].astype(F32)
                    fresh.append((jnp.sum(q * k, axis=1, keepdims=True), v))
                top = fresh[0][0]
                for score, _ in fresh[1:]:
                    top = jnp.maximum(top, score)
                for part in tops:
                    top = jnp.maximum(top, part[rows])
                total = jnp.zeros((8, 1), F32)
                out = jnp.zeros((8, 128), F32)
                for score, v in fresh:
                    w = jnp.exp2(score - top)
                    total += w
                    out += w.astype(BF).astype(F32) * v
                for n in range(8):
                    w = jnp.exp2(tops[n][rows] - top)
                    total += w * sums[n][rows]
                    out += w * parts[n, rows, cols]
                out_ref[rows, cols] = (out / total).astype(BF)


def merge_parts(parts, qkv_rows):
    return pl.pallas_call(
        merge_kernel,
        out_shape=jax.ShapeDtypeStruct((32, 256), BF),
        in_specs=[vmem_spec()] * 2,
        out_specs=vmem_spec(),
        compiler_params=pltpu.CompilerParams(vmem_limit_bytes=4 * MIB),
        cost_estimate=pl.CostEstimate(flops=MIB, bytes_accessed=MIB, transcendentals=1000),
        name="merge_parts",
    )(parts, qkv_rows)


def head_order_kernel(idx, a, b, c, d, near, far, out_ref):
    for k, piece in enumerate((a, b, c, d)):
        column = pl.multiple_of(lax.rem(idx[1] + k - 2 * idx[0] + 4, 4) * 128, 128)
        out_ref[:HALF, pl.ds(column, 128)] = piece[...]
    out_ref[HALF:, :256] = near[...]
    out_ref[HALF:, 256:] = far[...]


def head_order(idx, pieces, near, far):
    return pl.pallas_call(
        head_order_kernel,
        out_shape=jax.ShapeDtypeStruct((ROWS, 512), BF),
        in_specs=[smem_spec()] + [vmem_spec()] * 6,
        out_specs=vmem_spec(),
        compiler_params=pltpu.CompilerParams(vmem_limit_bytes=4 * MIB),
        cost_estimate=pl.CostEstimate(flops=0, bytes_accessed=MIB, transcendentals=0),
        name="head_order",
    )(idx, *pieces, near, far)


def out_kernel(step, idx, *refs):
    chips, parts = STEPS_OF[step]
    count = (4, 3, 2)[step]
    pieces, ws, refs = refs[:count], refs[count : count + 4], refs[count + 4 :]
    totals, refs = (refs[:2], refs[2:]) if step else (None, refs)
    results, xs = refs[:2], refs[2]
    for n, row, place, start, size in parts:
        xs[start : start + size, place * 512 : (place + 1) * 512] = pieces[n][row : row + size, :]
    for rel in range(2):
        side = idx[0] if rel == 0 else 1 - idx[0]
        columns = pl.ds(pl.multiple_of(side * 256, 256), 256)
        result = None if totals is None else totals[rel][...]
        for place, (dx, dy) in enumerate(chips):
            k = -dy % 4
            for half, w in enumerate(ws[2 * dx : 2 * dx + 2]):
                at = place * 512 + half * 256
                term = jnp.dot(
                    xs[:, at : at + 256],
                    w[k * 256 : (k + 1) * 256, columns],
                    preferred_element_type=F32,
                )
                result = term if result is None else result + term
        results[rel][...] = result


def out_project(step, idx, pieces, weights, totals=()):
    chips = len(STEPS_OF[step][0])
    return pl.pallas_call(
        functools.partial(out_kernel, step),
        out_shape=(
            jax.ShapeDtypeStruct((ROWS, 256), F32),
            jax.ShapeDtypeStruct((ROWS, 256), F32),
        ),
        in_specs=[smem_spec()] + [vmem_spec()] * (len(pieces) + 4 + len(totals)),
        out_specs=(vmem_spec(), vmem_spec()),
        scratch_shapes=[pltpu.VMEM((ROWS, chips * 512), BF)],
        compiler_params=pltpu.CompilerParams(vmem_limit_bytes=20 * MIB),
        cost_estimate=pl.CostEstimate(
            flops=2 * ROWS * 512 * chips * 512, bytes_accessed=4 * MIB, transcendentals=0
        ),
        name="out_project",
    )(idx, *pieces, *weights, *totals)


def pick(pair, core):
    return jnp.where(core == 0, pair[0], pair[1])


def shards(
    prompt,
    decode_tokens,
    query_weight,
    key_weight,
    value_weight,
    out_weight,
    cache_keys,
    cache_values,
    stretch_lengths,
    panel_map,
    ctx_lengths,
):
    inst = lax.axis_index("inst")
    tp = lax.axis_index("tp")
    core = tp % 2
    y = (tp // 2) % 4
    x = tp // 8
    z = inst % 4
    xh = inst // 4
    idx = jnp.stack([core, z, x, y, xh, inst, 0, 0]).astype(jnp.int32)

    groups = prompt.reshape(2, 2, GROUP, 256)
    tokens = decode_tokens.reshape(STEPS, 2, 8, 256)
    halves = [
        jnp.concatenate(
            [groups[:, n].reshape(HALF, 256), tokens[:, n].reshape(DEC, 256)], axis=0
        )
        for n in range(2)
    ]
    mine, theirs = pick(halves, core), pick(halves[::-1], core)
    received = move(theirs, dc=1)
    query_w, key_w, received = lax.optimization_barrier((query_weight, key_weight, received))
    first = gather_first(jnp.concatenate([mine, received], axis=1))
    sib_query, sib_key = move(query_w, dc=1), move(key_w, dc=1)
    value_w, *rest = lax.optimization_barrier((value_weight, *first[1:]))
    first = (first[0], *rest)
    sib_value = move(value_w, dc=1)
    second = gather_second(first)
    weights = (query_weight, key_weight, value_weight, sib_query, sib_key, sib_value)
    total = qkv(0, idx, first, weights)
    total, *second = lax.optimization_barrier((total, *second))
    third = gather_third(second)
    total = qkv(1, idx, second, weights, (total,))
    own_rows, *by_head, rows_out = qkv(2, idx, third, weights, (total,))

    heads = [move(by_head[k], dz=k) for k in (1, 3, 2)]
    one, three, two, own = lax.optimization_barrier((*heads, by_head[0]))
    blocks = (own, one, two, three)
    mine = pack(blocks)
    cross = move(mine, dxh=1, only_xh=0)
    queries = jnp.stack([a[HALF:, :256].reshape(2, DEC, 256) for a in blocks])
    other_queries = move(queries, dxh=1)
    sib = move(mine, dc=1)

    rows_out, queries, other_queries, out_w = lax.optimization_barrier(
        (rows_out, queries, other_queries, out_weight)
    )
    queries = jnp.concatenate([queries, other_queries], axis=0)
    pair = (queries[:, 0], move(queries[:, 1], dc=1))
    from_sib = move(rows_out, dc=1)
    queries = jnp.concatenate([pick(pair, core), pick(pair[::-1], core)], axis=1)
    queries = queries.reshape(256, 256)
    pair = (own_rows[HALF:], from_sib[HALF:])
    dec_rows = jnp.concatenate([pick(pair, core), pick(pair[::-1], core)], axis=0)

    spread = []
    for dy in range(4):
        at = (y + dy) % 4 * 512
        columns = jnp.concatenate(
            [
                lax.dynamic_slice_in_dim(out_w, side * 2048 + at, 512, axis=1)
                for side in (x, 1 - x)
            ],
            axis=1,
        )
        spread.append(columns if dy == 0 else move(columns, dy=dy))

    positions = (
        panel_map[:, :, None] * PANEL + jnp.arange(PANEL, dtype=jnp.int32)[None, None, :]
    )
    ok = (positions < ctx_lengths[:, None, None]).astype(F32).reshape(8, CH)
    parts = decode_parts(
        idx, stretch_lengths, queries, cache_keys, cache_values, ok, own_rows, from_sib
    )
    moved = move(parts[4:], dxh=1)
    parts, mine = lax.optimization_barrier((parts, mine))
    state = attend_own(idx, stretch_lengths, blocks, mine, sib)
    acc, top, *spread = lax.optimization_barrier((*state, *spread))
    acc, top, moved, cross, near, far = lax.optimization_barrier(
        (acc, top, moved, cross, *pack_weight(spread))
    )
    state = (acc, top)
    cross_sib = move(cross, dc=1)
    parts = jnp.stack([parts[:4], moved])
    moved = [move(parts[:, k], dz=4 - k) for k in (1, 2, 3)]
    far = move(far, dxl=1)
    first_heads = attend_cross(
        (1, 2, 3), idx, stretch_lengths, blocks[1:], cross, cross_sib, state
    )
    first_heads, *moved = lax.optimization_barrier((first_heads, *moved))
    back_one = move(first_heads[0], dz=3)
    back_two = move(first_heads[1], dz=2)
    back_three = move(first_heads[2], dz=1)
    parts = jnp.stack([parts[:, 0], *moved], axis=1).reshape(8, 32, 384)
    dec_attn = merge_parts(parts, dec_rows)
    theirs = move(pick((dec_attn[DEC:], dec_attn[:DEC]), core), dc=1)
    dec_attn, cross = lax.optimization_barrier((dec_attn, cross))
    mine = pick((dec_attn[:DEC], dec_attn[DEC:]), core)
    last_heads = attend_cross((0,), idx, stretch_lengths, (own,), cross, cross_sib, state)
    near, last_heads = lax.optimization_barrier((near, last_heads))
    attn = head_order(idx, (last_heads[0], back_one, back_two, back_three), mine, theirs)
    first = gather_first(attn)
    attn, near = lax.optimization_barrier((attn, near))
    weights = (near, move(near, dc=1), far, move(far, dc=1))
    second = gather_second(first)
    totals = out_project(0, idx, first, weights)
    *totals, up, down, across = lax.optimization_barrier((*totals, *second))
    second = (up, down, across)
    third = gather_third(second)
    totals = out_project(1, idx, second, weights, totals)
    mine, theirs = out_project(2, idx, third, weights, totals)
    received = move(theirs, dc=1)
    pair = (mine, received)
    sides = [pick(pair, core), pick(pair[::-1], core)]
    prefill_out = jnp.stack(
        [side[:HALF].reshape(2, GROUP, 256) for side in sides], axis=1
    ).reshape(CH, 256)
    decode_out = jnp.stack(
        [side[HALF:].reshape(STEPS, 8, 256) for side in sides], axis=1
    ).reshape(STEPS, 16, 256)
    return prefill_out, decode_out


def solution(mesh):
    return jax.shard_map(
        shards,
        mesh=mesh,
        in_specs=(
            P("inst", "tp"),
            P(None, "inst", "tp"),
            P(None, "tp"),
            P(None, "tp"),
            P(None, "tp"),
            P("tp", None),
            P(None, "inst", None, "tp"),
            P(None, "inst", None, "tp"),
            P(),
            P(None, "inst"),
            P(),
        ),
        out_specs=(P("inst", "tp"), P(None, "inst", "tp")),
        check_vma=False,
    )
```
